32 devices in a mesh: leaf: 8 (over z, x), col: 4 (over y, core).
Axes of the slice: x: 2, y: 2, z: 4, core: 2. Of those that a mesh axis runs over, the one named last changes fastest.
Arguments:
- leaf_rhs: bfloat16 [256, 256, 512], P('leaf', None, 'col'), may hold values from -6 to 6
- leaf_lower_inv: bfloat16 [256, 256, 256], P(('leaf', 'col')), may hold values from -0.375 to 0.375
- leaf_lower_panels: bfloat16 [256, 3, 256, 256], P(('leaf', 'col')), may hold values from -0.03125 to 0.03125
- leaf_upper_inv: bfloat16 [256, 256, 256], P(('leaf', 'col')), may hold values from -0.375 to 0.375
- leaf_upper_panels: bfloat16 [256, 3, 256, 256], P(('leaf', 'col')), may hold values from -0.21875 to 0.21875
- ancestors: int32 [256, 3], P(('leaf', 'col')), may hold values from 0 to 3
- sep_rhs: bfloat16 [8, 256, 512], P('leaf', None, 'col'), may hold values from -6 to 6
- sep_lower_inv: bfloat16 [8, 256, 256], P('leaf'), may hold values from -0.375 to 0.375
- sep_lower_panels: bfloat16 [8, 2, 256, 256], P('leaf'), may hold values from -0.109375 to 0.109375
- sep_upper_inv: bfloat16 [8, 256, 256], P('leaf'), may hold values from -0.375 to 0.375
- sep_upper_panels: bfloat16 [8, 2, 256, 256], P('leaf'), may hold values from -0.21875 to 0.21875
Outputs:
- leaf_solution: bfloat16 [256, 256, 512], P('leaf', None, 'col')
- sep_solution: bfloat16 [8, 256, 512], P('leaf', None, 'col')
The draws below stay inside these ranges and needn't reach their ends.
Inputs may be any that keep to these rules, and one draw needn't show every extreme that they name: `ancestors`: 0 marks an empty slot; a value m names the separator of level m above the supernode's subtree; a row may name a level more than once.
All inputs are finite; a program needn't handle non-finite values.
Results may differ from the reference program's by a relative error of at most 0.022.
Values may be sent and summed in bfloat16 or wider, within the bound.
No kernel may reach another device: no remote copies, remote signals or barrier semaphores. Data moves between devices by JAX's collectives and lax.ppermute only.
A program may use at most 128 MiB of HBM per device.

```python
import jax
import jax.numpy as jnp
from jax import lax

B = 256
R = 512
SD = 32
A = 3
H = 3
LEAVES = 256
N_LEAF = 8


def place_ends(result, own_key, least, largest):
    index_at = [jax.random.randint(jax.random.fold_in(own_key, axis), (), 0, length) for axis, length in enumerate(result.shape)]
    main_axis = result.shape.index(max(result.shape))
    neighbour = index_at[:main_axis] + [(index_at[main_axis] + 1) % result.shape[main_axis]] + index_at[main_axis + 1:]
    return result.at[tuple(index_at)].set(least).at[tuple(neighbour)].set(largest)


def shard_levels(stream_key, dims, pieces, smallest, largest):
    def one(position, blocks):
        draws = jax.random.uniform(jax.random.fold_in(jax.random.fold_in(stream_key, 6), position), (blocks,), jnp.float32, smallest / len(pieces), largest / len(pieces))
        return jnp.repeat(jnp.exp(draws), dims[position] // blocks).reshape((-1,) + (1,) * (len(dims) - position - 1))

    loudness = one(*pieces[0])
    for cut in pieces[1:]:
        loudness = loudness * one(*cut)
    return loudness


def centred(stream_key, extent, spread, limit, split=(), kind=jnp.bfloat16):
    drawn = jax.random.normal(stream_key, extent, jnp.float32) * spread
    if len(split) > 0:
        drawn = shard_levels(stream_key, extent, split, -0.22, 0.18) * drawn
    return jnp.clip(drawn, min=-limit, max=limit).astype(kind)


def setup_inputs(seed: int = 0) -> dict:
    splits = jax.random.split(jax.random.key(seed), 12)
    return {
        "leaf_rhs": centred(splits[0], (LEAVES, B, R), 1.0, 6.0, ((0, 8), (2, 4))),
        "leaf_lower_inv": centred(splits[1], (LEAVES, B, B), B ** -0.5, 0.375, ((0, 32),)),
        "leaf_lower_panels": centred(splits[2], (LEAVES, A, B, B), (4 * B * SD) ** -0.5, 0.03125, ((0, 32),)),
        "leaf_upper_inv": centred(splits[3], (LEAVES, B, B), B ** -0.5, 0.375, ((0, 32),)),
        "leaf_upper_panels": centred(splits[4], (LEAVES, A, B, B), (A * B) ** -0.5, 0.21875, ((0, 32),)),
        "ancestors": place_ends(jax.random.randint(splits[5], (LEAVES, A), 0, H + 1), jax.random.fold_in(splits[5], 1), 0, H).astype(jnp.int32),
        "sep_rhs": centred(splits[6], (N_LEAF, B, R), 1.0, 6.0, ((0, 8), (2, 4))),
        "sep_lower_inv": centred(splits[7], (N_LEAF, B, B), B ** -0.5, 0.375, ((0, 8),)),
        "sep_lower_panels": centred(splits[8], (N_LEAF, H - 1, B, B), (4 * B * H) ** -0.5, 0.109375, ((0, 8),)),
        "sep_upper_inv": centred(splits[9], (N_LEAF, B, B), B ** -0.5, 0.375, ((0, 8),)),
        "sep_upper_panels": centred(splits[10], (N_LEAF, H - 1, B, B), (B * H) ** -0.5, 0.21875, ((0, 8),)),
    }


HIGH = lax.Precision.HIGHEST


def sep_row(height, device):
    return jnp.left_shift(jnp.right_shift(device, height), height) + jnp.left_shift(jnp.int32(1), height - 1)


def leaf_forward(items):
    rhs_block, lower_inv, lower_panels, chosen = items
    leaf_value = jnp.einsum("kbc,kcr->kbr", lower_inv.astype(jnp.float32), rhs_block.astype(jnp.float32), precision=HIGH).astype(jnp.bfloat16)
    products = jnp.einsum("kabc,kcr->kabr", lower_panels.astype(jnp.float32), leaf_value.astype(jnp.float32), precision=HIGH)
    partial_value = jnp.einsum("kal,kabr->lbr", chosen, products, precision=HIGH)
    return leaf_value, partial_value


def reference(leaf_rhs, leaf_lower_inv, leaf_lower_panels, leaf_upper_inv, leaf_upper_panels, ancestors, sep_rhs, sep_lower_inv, sep_lower_panels, sep_upper_inv, sep_upper_panels):
    heights = jnp.arange(1, H + 1, dtype=jnp.int32)
    devices = jnp.arange(N_LEAF, dtype=jnp.int32)
    chosen = (ancestors[:, :, None] == heights[None, None, :]).astype(jnp.float32).reshape(N_LEAF, SD, A, H)
    leaf_value, partial_value = lax.map(leaf_forward, (leaf_rhs.reshape(N_LEAF, SD, B, R), leaf_lower_inv.reshape(N_LEAF, SD, B, B), leaf_lower_panels.reshape(N_LEAF, SD, A, B, B), chosen))
    targets = sep_row(heights[None, :], devices[:, None]).reshape(-1)
    pending = jnp.zeros((N_LEAF, B, R), jnp.float32).at[targets].add(partial_value.reshape(N_LEAF * H, B, R))
    sep_forward = jnp.zeros((N_LEAF, B, R), jnp.bfloat16)
    for height in range(1, H + 1):
        tier_rows = jnp.arange(2 ** (height - 1), N_LEAF, 2 ** height, dtype=jnp.int32)
        sep_input = (sep_rhs[tier_rows].astype(jnp.float32) - pending[tier_rows]).astype(jnp.bfloat16)
        sep_value = jnp.einsum("nbc,ncr->nbr", sep_lower_inv[tier_rows].astype(jnp.float32), sep_input.astype(jnp.float32), precision=HIGH).astype(jnp.bfloat16)
        sep_forward = sep_forward.at[tier_rows].set(sep_value)
        for slot_index in range(H - height):
            target_rows = sep_row(jnp.int32(height + 1 + slot_index), tier_rows)
            update = jnp.einsum("nbc,ncr->nbr", sep_lower_panels[tier_rows, slot_index].astype(jnp.float32), sep_value.astype(jnp.float32), precision=HIGH)
            pending = pending.at[target_rows].add(update)
    sep_solution = jnp.zeros((N_LEAF, B, R), jnp.bfloat16)
    for height in range(H, 0, -1):
        tier_rows = jnp.arange(2 ** (height - 1), N_LEAF, 2 ** height, dtype=jnp.int32)
        remaining = sep_forward[tier_rows].astype(jnp.float32)
        for slot_index in range(H - height):
            source_rows = sep_row(jnp.int32(height + 1 + slot_index), tier_rows)
            remaining = remaining - jnp.einsum("nbc,ncr->nbr", sep_upper_panels[tier_rows, slot_index].astype(jnp.float32), sep_solution[source_rows].astype(jnp.float32), precision=HIGH)
        sep_rest = remaining.astype(jnp.bfloat16)
        solved_tier = jnp.einsum("nbc,ncr->nbr", sep_upper_inv[tier_rows].astype(jnp.float32), sep_rest.astype(jnp.float32), precision=HIGH).astype(jnp.bfloat16)
        sep_solution = sep_solution.at[tier_rows].set(solved_tier)

    def leaf_backward(items):
        value_block, upper_inv, upper_panels, picked_levels, device = items
        path_values = sep_solution[sep_row(heights, device)].astype(jnp.float32)
        picked = jnp.einsum("kal,lbr->kabr", picked_levels, path_values, precision=HIGH)
        update = jnp.einsum("kabc,kacr->kbr", upper_panels.astype(jnp.float32), picked, precision=HIGH)
        leaf_rest = (value_block.astype(jnp.float32) - update).astype(jnp.bfloat16)
        return jnp.einsum("kbc,kcr->kbr", upper_inv.astype(jnp.float32), leaf_rest.astype(jnp.float32), precision=HIGH).astype(jnp.bfloat16)

    leaf_solution = lax.map(leaf_backward, (leaf_value, leaf_upper_inv.reshape(N_LEAF, SD, B, B), leaf_upper_panels.reshape(N_LEAF, SD, A, B, B), chosen, devices))
    return leaf_solution.reshape(N_LEAF * SD, B, R), sep_solution
```

```python
import functools

import jax
import jax.numpy as jnp
from jax import lax
from jax.experimental import pallas as pl
from jax.experimental.pallas import tpu as pltpu
from jax.sharding import PartitionSpec as P

F32 = jnp.float32
BF16 = jnp.bfloat16
VMEM_LIMIT = 48 * 2**20


def swap(value, axis, mask):
    pairs = [(source, source ^ mask) for source in range(lax.axis_size(axis))]
    return lax.ppermute(value, axis, pairs)


def dot(left, right):
    return jnp.dot(left, right, preferred_element_type=F32)


def params():
    return pltpu.CompilerParams(vmem_limit_bytes=VMEM_LIMIT)


def cost(flops, moved):
    return pl.CostEstimate(flops=flops, bytes_accessed=moved, transcendentals=0)


def forward_kernel(levels, offsets, ancestors, rhs, inv, panels, start, value, total, held):
    step = pl.program_id(0)
    slots = panels.shape[1]

    @pl.when(step == 0)
    def _():
        held[...] = start[...]

    solved = dot(inv[0], rhs[0]).astype(BF16)
    value[0] = solved
    products = [dot(panels[0, slot], solved) for slot in range(slots)]
    for level in range(levels):
        add = None
        for slot in range(slots):
            chosen = (ancestors[step, slot] == level + 1).astype(F32)
            term = products[slot] * chosen
            add = term if add is None else add + term
        held[level] += add

    @pl.when(step == pl.num_programs(0) - 1)
    def _():
        total[...] = held[...].astype(total.dtype)


def forward(offset, ancestors, rhs, inv, panels, start, out_dtype):
    count, size, _ = inv.shape
    slots = panels.shape[1]
    levels, _, cols = start.shape
    return pl.pallas_call(
        functools.partial(forward_kernel, levels),
        grid_spec=pltpu.PrefetchScalarGridSpec(
            num_scalar_prefetch=2,
            grid=(count,),
            in_specs=[
                pl.BlockSpec((1, size, cols), lambda i, offsets, _: (offsets[0] + i, 0, 0)),
                pl.BlockSpec((1, size, size), lambda i, *_: (i, 0, 0)),
                pl.BlockSpec((1, slots, size, size), lambda i, *_: (i, 0, 0, 0)),
                pl.BlockSpec((levels, size, cols), lambda i, *_: (0, 0, 0)),
            ],
            out_specs=[
                pl.BlockSpec((1, size, cols), lambda i, *_: (i, 0, 0)),
                pl.BlockSpec((levels, size, cols), lambda i, *_: (0, 0, 0)),
            ],
            scratch_shapes=[pltpu.VMEM((levels, size, cols), F32)],
        ),
        out_shape=[
            jax.ShapeDtypeStruct((count, size, cols), BF16),
            jax.ShapeDtypeStruct((levels, size, cols), out_dtype),
        ],
        compiler_params=params(),
        cost_estimate=cost(
            2 * count * (1 + slots) * size * size * cols,
            2 * count * size * ((1 + slots) * size + 2 * cols),
        ),
        name="leaf_forward",
    )(offset, ancestors, rhs, inv, panels, start)


def backward_kernel(ancestors, value, inv, panels, paths, result):
    step = pl.program_id(0)
    rest = value[0].astype(F32)
    for slot in range(panels.shape[1]):
        level = ancestors[step, slot]
        picked = paths[jnp.maximum(level - 1, 0)]
        picked = jnp.where(level > 0, picked, jnp.zeros_like(picked))
        rest = rest - dot(panels[0, slot], picked)
    result[0] = dot(inv[0], rest.astype(BF16)).astype(BF16)


def backward(ancestors, value, inv, panels, paths):
    count, size, _ = inv.shape
    slots = panels.shape[1]
    levels, _, cols = paths.shape
    return pl.pallas_call(
        backward_kernel,
        grid_spec=pltpu.PrefetchScalarGridSpec(
            num_scalar_prefetch=1,
            grid=(count,),
            in_specs=[
                pl.BlockSpec((1, size, cols), lambda i, *_: (i, 0, 0)),
                pl.BlockSpec((1, size, size), lambda i, *_: (i, 0, 0)),
                pl.BlockSpec((1, slots, size, size), lambda i, *_: (i, 0, 0, 0)),
                pl.BlockSpec((levels, size, cols), lambda i, *_: (0, 0, 0)),
            ],
            out_specs=pl.BlockSpec((1, size, cols), lambda i, *_: (i, 0, 0)),
        ),
        out_shape=jax.ShapeDtypeStruct((count, size, cols), BF16),
        compiler_params=params(),
        cost_estimate=cost(
            2 * count * (1 + slots) * size * size * cols,
            2 * count * size * ((1 + slots) * size + 2 * cols),
        ),
        name="leaf_backward",
    )(ancestors, value, inv, panels, paths)


def climb_kernel(mine, theirs, factors, solved, passed):
    pending = mine[0].astype(F32) + theirs[0].astype(F32)
    value = dot(factors[0], (-pending).astype(BF16)).astype(BF16)
    solved[...] = value
    for above in range(passed.shape[0]):
        carried = mine[above + 1].astype(F32) + theirs[above + 1].astype(F32)
        passed[above] = (carried + dot(factors[2 + 2 * above], value)).astype(BF16)


def climb(mine, theirs, factors):
    levels, size, cols = mine.shape
    return pl.pallas_call(
        climb_kernel,
        out_shape=[
            jax.ShapeDtypeStruct((size, cols), BF16),
            jax.ShapeDtypeStruct((levels - 1, size, cols), BF16),
        ],
        compiler_params=params(),
        cost_estimate=cost(2 * levels * size * size * cols, 2 * levels * size * (size + 4 * cols)),
        name="climb",
    )(mine, theirs, factors)


def descend_kernel(levels, mine, theirs, *refs):
    factors, values, paths = refs[:levels], refs[levels : 2 * levels - 1], refs[-1]
    pending = mine[0].astype(F32) + theirs[0].astype(F32)
    top = dot(factors[levels - 1][0], (-pending).astype(BF16)).astype(BF16)
    for level in range(levels - 1, -1, -1):
        rest = top if level == levels - 1 else values[level][...]
        if level < levels - 1:
            rest = rest.astype(F32)
            for above in range(levels - 1 - level):
                rest = rest - dot(factors[level][3 + 2 * above], paths[level + 1 + above])
            rest = rest.astype(BF16)
        paths[level] = dot(factors[level][1], rest).astype(BF16)


def descend(mine, theirs, factors, values):
    levels = len(factors)
    _, size, cols = mine.shape
    return pl.pallas_call(
        functools.partial(descend_kernel, levels),
        out_shape=jax.ShapeDtypeStruct((levels, size, cols), BF16),
        compiler_params=params(),
        cost_estimate=cost(
            levels * (levels + 3) * size * size * cols, levels * (levels + 3) * size * size
        ),
        name="descend",
    )(mine, theirs, *factors, *values)


def along_path(own, levels, device):
    chosen = []
    for level in range(1, levels + 1):
        block = own[: 2 + 2 * (levels - level)]
        owner = 2 ** (level - 1)
        holders = {owner}
        for bit in reversed(range(level)):
            targets = {holder ^ 2**bit for holder in holders}
            groups = range(0, lax.axis_size("leaf"), 2**level)
            pairs = [(group + holder, group + (holder ^ 2**bit)) for group in groups for holder in sorted(holders)]
            arrived = lax.ppermute(block, "leaf", pairs)
            place = device % 2**level
            took = functools.reduce(jnp.logical_or, [place == target for target in sorted(targets)])
            block = jnp.where(took, arrived, block)
            holders |= targets
        chosen.append(block)
    return chosen


def on_device(
    leaf_rhs,
    leaf_lower_inv,
    leaf_lower_panels,
    leaf_upper_inv,
    leaf_upper_panels,
    ancestors,
    sep_rhs,
    sep_lower_inv,
    sep_lower_panels,
    sep_upper_inv,
    sep_upper_panels,
):
    levels = lax.axis_size("leaf").bit_length() - 1
    device = lax.axis_index("leaf")
    place = lax.axis_index("col")
    low, high = place % 2, place // 2
    count = leaf_lower_inv.shape[0]
    _, size, cols = leaf_rhs.shape

    first_rows = high * 2 * count + low * count
    second_rows = high * 2 * count + (1 - low) * count
    far_first_rows = (1 - high) * 2 * count + low * count
    far_second_rows = (1 - high) * 2 * count + (1 - low) * count
    far_first = swap(lax.dynamic_slice_in_dim(leaf_rhs, far_first_rows, count, 0), "col", 2)
    far_second = swap(lax.dynamic_slice_in_dim(leaf_rhs, far_second_rows, count, 0), "col", 2)
    near_ancestors = swap(ancestors, "col", 1)
    near_lower_inv = swap(leaf_lower_inv, "col", 1)
    near_lower_panels = swap(leaf_lower_panels, "col", 1)
    near_upper_inv = swap(leaf_upper_inv, "col", 1)
    near_upper_panels = swap(leaf_upper_panels, "col", 1)

    pieces = [sep_lower_inv, sep_upper_inv]
    for above in range(levels - 1):
        pieces += [sep_lower_panels[:, above], sep_upper_panels[:, above]]
    path_factors = along_path(jnp.concatenate(pieces, axis=0), levels, device)

    owned = [device % 2**level == 2 ** (level - 1) for level in range(1, levels + 1)]
    negated = -sep_rhs[0].astype(F32)
    start_own = jnp.stack([jnp.where(is_owner, negated, 0.0) for is_owner in owned])
    start_far = jnp.zeros_like(start_own)
    zero = jnp.zeros((1,), jnp.int32)

    def at(rows):
        return jnp.reshape(rows, (1,)).astype(jnp.int32)

    value_first, total = forward(
        at(first_rows), ancestors, leaf_rhs, leaf_lower_inv, leaf_lower_panels, start_own, F32
    )
    value_second, own_total = forward(
        at(second_rows), near_ancestors, leaf_rhs, near_lower_inv, near_lower_panels, total, F32
    )
    far_value_first, total = forward(
        zero, ancestors, far_first, leaf_lower_inv, leaf_lower_panels, start_far, F32
    )
    far_value_second, far_total = forward(
        zero, near_ancestors, far_second, near_lower_inv, near_lower_panels, total, BF16
    )

    mine = (own_total + swap(far_total, "col", 2).astype(F32)).astype(BF16)
    values = []
    for level in range(1, levels):
        theirs = swap(mine, "leaf", 2 ** (level - 1))
        solved, mine = climb(mine, theirs, path_factors[level - 1])
        values.append(solved)
    theirs = swap(mine, "leaf", 2 ** (levels - 1))
    paths = descend(mine, theirs, path_factors, values)
    far_paths = swap(paths, "col", 2)

    own_solution = jnp.zeros((size, cols), BF16)
    for level in range(levels):
        own_solution = jnp.where(owned[level], paths[level], own_solution)

    sent_first = backward(ancestors, far_value_first, leaf_upper_inv, leaf_upper_panels, far_paths)
    sent_second = backward(
        near_ancestors, far_value_second, near_upper_inv, near_upper_panels, far_paths
    )
    got_first = swap(sent_first, "col", 2)
    got_second = swap(sent_second, "col", 2)
    own_first = backward(ancestors, value_first, leaf_upper_inv, leaf_upper_panels, paths)
    own_second = backward(near_ancestors, value_second, near_upper_inv, near_upper_panels, paths)

    solution_rows = jnp.zeros(leaf_rhs.shape, BF16)
    for rows, part in (
        (first_rows, own_first),
        (second_rows, own_second),
        (far_first_rows, got_first),
        (far_second_rows, got_second),
    ):
        solution_rows = lax.dynamic_update_slice_in_dim(solution_rows, part, rows, 0)
    return (solution_rows, own_solution[None])


def solution(mesh):
    placed = (
        P("leaf", None, "col"),
        P(("leaf", "col"), None, None),
        P(("leaf", "col"), None, None, None),
        P(("leaf", "col"), None, None),
        P(("leaf", "col"), None, None, None),
        P(("leaf", "col"), None),
        P("leaf", None, "col"),
        P("leaf", None, None),
        P("leaf", None, None, None),
        P("leaf", None, None),
        P("leaf", None, None, None),
    )
    return jax.shard_map(
        on_device,
        mesh=mesh,
        in_specs=placed,
        out_specs=(P("leaf", None, "col"), P("leaf", None, "col")),
        check_vma=False,
    )
```

```python
import functools

import jax
import jax.numpy as jnp
from jax import lax
from jax.experimental import pallas as pl
from jax.experimental.pallas import tpu as pltpu
from jax.sharding import PartitionSpec as P

F32 = jnp.float32
BF16 = jnp.bfloat16
FORWARD_VMEM = 60 * 2**20
LEAF_VMEM = 10 * 2**20
TREE_VMEM = 6 * 2**20
BATCH = 4
PART = 3


def swap(value, axis, mask):
    pairs = [(source, source ^ mask) for source in range(lax.axis_size(axis))]
    return lax.ppermute(value, axis, pairs)


def dot(left, right):
    return jnp.dot(left, right, preferred_element_type=F32)


def cost(flops, moved):
    return pl.CostEstimate(flops=flops, bytes_accessed=moved, transcendentals=0)


def forward_kernel(first, last, scalars, ancestors, rhs, far, inv, panels, start, *refs):
    if last:
        value, own_total, far_total, solved, held, sems = refs
    else:
        value, total, solved, held, sems = refs
    step, steps = pl.program_id(0), pl.num_programs(0)
    batch, slots = panels.shape[:2]
    levels, _, both = held.shape
    cols = both // 2

    def leaving(leaf):
        return pltpu.make_async_copy(solved.at[leaf], value.at[leaf], sems.at[leaf])

    @pl.when(step == 0)
    def _():
        if first:
            for level in range(levels):
                held[level, :, :cols] = start[0].astype(F32) * -(scalars[2] == level + 1).astype(F32)
                held[level, :, cols:] = jnp.zeros((held.shape[1], cols), F32)
        else:
            held[...] = start[...]

    values = []
    for leaf in range(batch):
        columns = jnp.concatenate([rhs[leaf], far[leaf]], axis=1)
        values.append(dot(inv[leaf], columns).astype(BF16))
        solved[step * batch + leaf] = values[leaf]
        leaving(step * batch + leaf).start()
    sums = [None] * levels
    for leaf in range(batch):
        for slot in range(slots):
            product = dot(panels[leaf, slot], values[leaf])
            named = ancestors[step * batch + leaf, slot]
            for level in range(levels):
                term = product * (named == level + 1).astype(F32)
                sums[level] = term if sums[level] is None else sums[level] + term
    for level in range(levels):
        held[level] += sums[level]

    @pl.when(step == steps - 1)
    def _():
        if last:
            own_total[...] = held[:, :, :cols]
            far_total[...] = held[:, :, cols:].astype(BF16)
        else:
            total[...] = held[...]
        for leaf in range(solved.shape[0]):
            leaving(leaf).wait()


def forward(levels, scalars, which, ancestors, inv, panels, rhs, far, start, first, last):
    count, size, _ = inv.shape
    cols = rhs.shape[2]
    slots = panels.shape[1]
    batch = min(BATCH, count)
    whole = lambda i, *_: (0, 0, 0)
    if last:
        sums = [jax.ShapeDtypeStruct((levels, size, cols), F32), jax.ShapeDtypeStruct((levels, size, cols), BF16)]
    else:
        sums = [jax.ShapeDtypeStruct((levels, size, 2 * cols), F32)]
    return pl.pallas_call(
        functools.partial(forward_kernel, first, last),
        grid_spec=pltpu.PrefetchScalarGridSpec(
            num_scalar_prefetch=2,
            grid=(count // batch,),
            in_specs=[
                pl.BlockSpec((batch, size, cols), lambda i, scalars, _: (scalars[which] // batch + i, 0, 0)),
                pl.BlockSpec((batch, size, cols), lambda i, *_: (i, 0, 0)),
                pl.BlockSpec((batch, size, size), lambda i, *_: (i, 0, 0)),
                pl.BlockSpec((batch, slots, size, size), lambda i, *_: (i, 0, 0, 0)),
                pl.BlockSpec(start.shape, whole),
            ],
            out_specs=[pl.BlockSpec(memory_space=pl.ANY)] + [pl.BlockSpec(part.shape, whole) for part in sums],
            scratch_shapes=[
                pltpu.VMEM((count, size, 2 * cols), BF16),
                pltpu.VMEM((levels, size, 2 * cols), F32),
                pltpu.SemaphoreType.DMA((count,)),
            ],
        ),
        out_shape=[jax.ShapeDtypeStruct((count, size, 2 * cols), BF16)] + sums,
        compiler_params=pltpu.CompilerParams(vmem_limit_bytes=FORWARD_VMEM),
        cost_estimate=cost(0, 0),
        name="leaf_forward",
    )(scalars, ancestors, rhs, far, inv, panels, start)


def solve_leaves(base, step, batch, ancestors, value, inv, panels, paths):
    leaves = [step * batch + index for index in range(batch)]
    rests = []
    for leaf in leaves:
        update = None
        for slot in range(panels.shape[1]):
            level = ancestors[base + leaf, slot]
            picked = paths[jnp.maximum(level - 1, 0)]
            picked = jnp.where(level > 0, picked, jnp.zeros_like(picked))
            term = dot(panels[leaf, slot], picked)
            update = term if update is None else update + term
        rests.append((value[leaf].astype(F32) - update).astype(BF16))
    return [dot(inv[leaf], rest).astype(BF16) for leaf, rest in zip(leaves, rests)]


def send_kernel(base, ancestors, value, inv, panels, paths, result):
    count = result.shape[0]
    batch = min(BATCH, count)

    @pl.loop(0, count // batch)
    def _(step):
        solutions = solve_leaves(base, step, batch, ancestors, value, inv, panels, paths)
        for index, solution_block in enumerate(solutions):
            result[step * batch + index] = solution_block


def solve_far(ancestors, inv, panels, value, paths, base, count):
    size, cols = paths.shape[1:]

    def part(array):
        block = (count,) + array.shape[1:]
        return pl.BlockSpec(block, lambda i: (base // count,) + (0,) * (array.ndim - 1))

    return pl.pallas_call(
        functools.partial(send_kernel, base),
        grid=(1,),
        in_specs=[
            pl.BlockSpec(memory_space=pltpu.SMEM),
            pl.BlockSpec((count, size, cols), lambda i: (base // count, 0, 1)),
            part(inv),
            part(panels),
            pl.BlockSpec(paths.shape, lambda i: (0, 0, 0)),
        ],
        out_specs=pl.BlockSpec((count, size, cols), lambda i: (0, 0, 0)),
        out_shape=jax.ShapeDtypeStruct((count, size, cols), BF16),
        compiler_params=pltpu.CompilerParams(vmem_limit_bytes=LEAF_VMEM),
        cost_estimate=cost(0, 0),
        name="solve_far",
    )(ancestors, value, inv, panels, paths)


def keep_kernel(which, scalars, ancestors, value, inv, panels, paths, *refs):
    result, solved, sems = refs[-3:]
    step, steps = pl.program_id(0), pl.num_programs(0)
    batch = value.shape[0]

    def leaving(leaf):
        return pltpu.make_async_copy(solved.at[leaf], result.at[scalars[which] + leaf], sems.at[leaf])

    for index, solution_block in enumerate(solve_leaves(step * batch, 0, batch, ancestors, value, inv, panels, paths)):
        solved[step * batch + index] = solution_block
        leaving(step * batch + index).start()

    @pl.when(step == steps - 1)
    def _():
        for leaf in range(solved.shape[0]):
            leaving(leaf).wait()


def solve_own(scalars, which, ancestors, inv, panels, value, paths, rows, into=None):
    size, cols = paths.shape[1:]
    count, slots = panels.shape[:2]
    batch = min(BATCH, count)
    extra = [] if into is None else [into]
    hbm, smem = pl.BlockSpec(memory_space=pl.ANY), pl.BlockSpec(memory_space=pltpu.SMEM)
    return pl.pallas_call(
        functools.partial(keep_kernel, which),
        grid=(count // batch,),
        in_specs=[
            smem,
            smem,
            pl.BlockSpec((batch, size, cols), lambda i: (i, 0, 0)),
            pl.BlockSpec((batch, size, size), lambda i: (i, 0, 0)),
            pl.BlockSpec((batch, slots, size, size), lambda i: (i, 0, 0, 0)),
            pl.BlockSpec(paths.shape, lambda i: (0, 0, 0)),
        ]
        + [hbm] * len(extra),
        out_specs=hbm,
        out_shape=jax.ShapeDtypeStruct((rows, size, cols), BF16),
        scratch_shapes=[pltpu.VMEM((count, size, cols), BF16), pltpu.SemaphoreType.DMA((count,))],
        input_output_aliases={} if into is None else {6: 0},
        compiler_params=pltpu.CompilerParams(vmem_limit_bytes=LEAF_VMEM),
        cost_estimate=cost(0, 0),
        name="solve_own",
    )(scalars, ancestors, value, inv, panels, paths, *extra)


def place_kernel(scalars, part, whole, result):
    result[...] = part[...]


def place_rows(scalars, which, offset, part, whole):
    count, size, cols = part.shape
    return pl.pallas_call(
        place_kernel,
        grid_spec=pltpu.PrefetchScalarGridSpec(
            num_scalar_prefetch=1,
            grid=(1,),
            in_specs=[pl.BlockSpec(part.shape, lambda i, _: (0, 0, 0)), pl.BlockSpec(memory_space=pl.ANY)],
            out_specs=pl.BlockSpec(part.shape, lambda i, scalars: ((scalars[which] + offset) // count, 0, 0)),
        ),
        out_shape=jax.ShapeDtypeStruct(whole.shape, whole.dtype),
        input_output_aliases={2: 0},
        compiler_params=pltpu.CompilerParams(vmem_limit_bytes=LEAF_VMEM),
        cost_estimate=cost(0, 0),
        name="place_rows",
    )(scalars, part, whole)


def combine_kernel(lower_inv, lower_panels, upper_inv, upper_panels, blocks, *parts):
    made = [dot(upper_inv[0], lower_inv[0]).astype(BF16)]
    for slot in range(blocks.shape[0] // 2):
        made.append(dot(lower_panels[0, slot], lower_inv[0]).astype(BF16))
        made.append(dot(upper_inv[0], upper_panels[0, slot]).astype(BF16))
    for index, block in enumerate(made):
        blocks[index] = block
    for part in parts:
        for index in range(part.shape[0]):
            part[index] = made.pop(0)


def combine(lower_inv, lower_panels, upper_inv, upper_panels):
    size = lower_inv.shape[1]
    total = 1 + 2 * lower_panels.shape[1]
    counts = [total] + [min(PART, total - begin) for begin in range(0, total, PART)]
    blocks, *parts = pl.pallas_call(
        combine_kernel,
        out_shape=[jax.ShapeDtypeStruct((blocks, size, size), BF16) for blocks in counts],
        compiler_params=pltpu.CompilerParams(vmem_limit_bytes=TREE_VMEM),
        cost_estimate=cost(2**20, 2**20),
        name="combine",
    )(lower_inv, lower_panels, upper_inv, upper_panels)
    return blocks, parts


def sort_kernel(parts, flags, mine, *refs):
    theirs, factors, rest = refs[:parts], refs[parts], refs[parts + 1 :]

    @pl.when(flags[0] == 1)
    def _():
        factors[...] = mine[...]
        for onward in rest:
            begin = 0
            for part in theirs:
                for index in range(min(part.shape[0], onward.shape[0] - begin)):
                    onward[begin + index] = part[index]
                begin += part.shape[0]

    @pl.when(flags[0] == 0)
    def _():
        begin = 0
        for part in theirs:
            factors[begin : begin + part.shape[0]] = part[...]
            begin += part.shape[0]
        for onward in rest:
            onward[...] = mine[: onward.shape[0]]


def sort(bit, mine, theirs):
    memory = pl.BlockSpec(memory_space=pltpu.VMEM)
    shapes = [jax.ShapeDtypeStruct(mine.shape, BF16)]
    if mine.shape[0] > 1:
        shapes.append(jax.ShapeDtypeStruct((mine.shape[0] - 2,) + mine.shape[1:], BF16))
        shapes.append(jax.ShapeDtypeStruct((1,) + mine.shape[1:], BF16))
    return pl.pallas_call(
        functools.partial(sort_kernel, len(theirs)),
        in_specs=[pl.BlockSpec(memory_space=pltpu.SMEM), memory] + [memory] * len(theirs),
        out_specs=[memory] * len(shapes),
        out_shape=shapes,
        compiler_params=pltpu.CompilerParams(vmem_limit_bytes=TREE_VMEM),
        cost_estimate=cost(2**20, 2**20),
        name="sort",
    )(jnp.reshape(bit, (1,)).astype(jnp.int32), mine, *theirs)


def pick_kernel(flags, *refs):
    sources, chosen = refs[:-1], refs[-1]
    for index, source in enumerate(sources):

        @pl.when(flags[0] == index)
        def _(source=source):
            chosen[...] = source[...]


def pick(index, sources):
    shape = (1,) + sources[0].shape[1:]
    return pl.pallas_call(
        pick_kernel,
        grid=(1,),
        in_specs=[pl.BlockSpec(memory_space=pltpu.SMEM)] + [pl.BlockSpec(shape, lambda i: (0, 0, 0))] * len(sources),
        out_specs=pl.BlockSpec(shape, lambda i: (0, 0, 0)),
        out_shape=jax.ShapeDtypeStruct(shape, BF16),
        compiler_params=pltpu.CompilerParams(vmem_limit_bytes=TREE_VMEM),
        cost_estimate=cost(2**20, 2**20),
        name="pick",
    )(jnp.reshape(index, (1,)).astype(jnp.int32), *sources)


def from_owners(value, level, hop):
    owner = 2 ** (level - 1)
    pairs = [
        (group + owner + index, group + (owner + index ^ hop))
        for group in range(0, lax.axis_size("leaf"), 2**level)
        for index in range(2)
    ]
    return lax.ppermute(value, "leaf", pairs)


def after(value, *earlier):
    return lax.optimization_barrier((value, *earlier))[0]


def climb_kernel(mine, theirs, factors, part, passed):
    entered = (-(mine[0].astype(F32) + theirs[0].astype(F32))).astype(BF16)
    for above in range(passed.shape[0]):
        carried = mine[above + 1].astype(F32) + theirs[above + 1].astype(F32)
        passed[above] = (carried + dot(factors[1 + 2 * above], entered)).astype(BF16)
    part[...] = dot(factors[0], entered)


def climb(mine, theirs, factors):
    levels, size, cols = mine.shape
    return pl.pallas_call(
        climb_kernel,
        out_shape=[
            jax.ShapeDtypeStruct((size, cols), F32),
            jax.ShapeDtypeStruct((levels - 1, size, cols), BF16),
        ],
        compiler_params=pltpu.CompilerParams(vmem_limit_bytes=TREE_VMEM),
        cost_estimate=cost(2**20, 2**20),
        name="climb",
    )(mine, theirs, factors)


def descend_kernel(levels, mine, theirs, *refs):
    factors, parts, paths = refs[:levels], refs[levels : 2 * levels - 1], refs[-1]
    entered = (-(mine[0].astype(F32) + theirs[0].astype(F32))).astype(BF16)
    paths[levels - 1] = dot(factors[levels - 1][0], entered).astype(BF16)
    for level in range(levels - 2, -1, -1):
        rest = parts[level][...]
        for above in reversed(range(levels - 1 - level)):
            rest = rest - dot(factors[level][2 + 2 * above], paths[level + 1 + above])
        paths[level] = rest.astype(BF16)


def descend(mine, theirs, factors, parts):
    levels = len(factors)
    _, size, cols = mine.shape
    return pl.pallas_call(
        functools.partial(descend_kernel, levels),
        out_shape=jax.ShapeDtypeStruct((levels, size, cols), BF16),
        compiler_params=pltpu.CompilerParams(vmem_limit_bytes=TREE_VMEM),
        cost_estimate=cost(2**20, 2**20),
        name="descend",
    )(mine, theirs, *factors, *parts)


def on_device(
    leaf_rhs,
    leaf_lower_inv,
    leaf_lower_panels,
    leaf_upper_inv,
    leaf_upper_panels,
    ancestors,
    sep_rhs,
    sep_lower_inv,
    sep_lower_panels,
    sep_upper_inv,
    sep_upper_panels,
):
    levels = lax.axis_size("leaf").bit_length() - 1
    device = lax.axis_index("leaf")
    place = lax.axis_index("col")
    low, high = place % 2, place // 2
    count = leaf_lower_inv.shape[0]
    rows, size, cols = leaf_rhs.shape

    first = high * 2 * count + low * count
    second = high * 2 * count + (1 - low) * count
    owned = [device % 2**level == 2 ** (level - 1) for level in range(1, levels + 1)]
    own_level = sum(jnp.where(is_owner, level, 0) for level, is_owner in enumerate(owned, 1))

    away = (1 - high) * 2 * count
    scalars = jnp.stack([first, second, own_level, away + low * count, away + (1 - low) * count]).astype(jnp.int32)
    half = count // 2
    sent = lax.optimization_barrier(
        [lax.dynamic_slice_in_dim(leaf_rhs, away + part * count, count, 0) for part in (low, 1 - low)]
    )
    far_rhs = [swap(part, "col", 2) for part in sent]

    near_ancestors = swap(ancestors, "col", 1)
    near_lower_inv = swap(leaf_lower_inv, "col", 1)
    near_lower_panels = swap(leaf_lower_panels, "col", 1)
    local = (ancestors, leaf_lower_inv, leaf_lower_panels)
    near = (near_ancestors, near_lower_inv, near_lower_panels)

    blocks, pieces = combine(after(sep_lower_inv, *sent), sep_lower_panels, sep_upper_inv, sep_upper_panels)

    start = after(sep_rhs, *near)
    value_1, total = forward(levels, scalars, 0, *local, leaf_rhs, far_rhs[0], start, True, False)
    arrived = [swap(piece, "leaf", 1) for piece in pieces]
    found, *onward = sort(device % 2, blocks, after(arrived, total))
    factors = [found]
    total = after(total, found)
    value_2, own_total, far_total = forward(levels, scalars, 1, *near, leaf_rhs, far_rhs[1], total, False, True)

    if levels == 3:
        from_top = [from_owners(onward[1], levels, hop) for hop in (4, 6)]
        far_total = after(far_total, *from_top)
    mine = (own_total + swap(far_total, "col", 2).astype(F32)).astype(BF16)
    parts = []
    for level in range(1, levels + 1):
        theirs = swap(mine, "leaf", 2 ** (level - 1))
        if onward:
            arrived = swap(onward[0], "leaf", 2**level)
            before = onward[0]
            found, *onward = sort(device // 2**level % 2, before, [arrived])
            factors.append(found)
            theirs = after(theirs, found)
            top = None
            if levels == 3:
                top = pick(device // 2 % 4, [*from_top, before, arrived])
                factors.append(top)
                onward = []
        elif level == 2:
            theirs = after(theirs, top)
        if level < levels:
            part, mine = climb(mine, theirs, factors[level - 1])
            parts.append(part)
        if level == 1:
            near_upper_inv = swap(after(leaf_upper_inv, mine), "col", 1)
            near_upper_panels = swap(after(leaf_upper_panels, mine), "col", 1)
    paths = descend(mine, theirs, factors, parts)
    far_paths = swap(paths, "col", 2)

    own_solution = jnp.zeros((size, cols), BF16)
    for level in range(levels):
        own_solution = jnp.where(owned[level], paths[level], own_solution)

    local = (ancestors, leaf_upper_inv, leaf_upper_panels)
    near = (near_ancestors, near_upper_inv, near_upper_panels)
    leaf_solution = solve_own(scalars, 0, *local, value_1, paths, rows)
    far_paths = after(far_paths, leaf_solution)
    returning = [
        (3, 0, solve_far(*local, value_1, far_paths, 0, count)),
        (4, 0, solve_far(*near, value_2, far_paths, 0, half)),
        (4, half, solve_far(*near, value_2, far_paths, half, half)),
    ]
    leaf_solution = solve_own(scalars, 1, *near, value_2, paths, rows, leaf_solution)
    for which, offset, part in returning:
        leaf_solution = place_rows(scalars, which, offset, swap(part, "col", 2), leaf_solution)
    return (leaf_solution, own_solution[None])


def solution(mesh):
    placed = (
        P("leaf", None, "col"),
        P(("leaf", "col"), None, None),
        P(("leaf", "col"), None, None, None),
        P(("leaf", "col"), None, None),
        P(("leaf", "col"), None, None, None),
        P(("leaf", "col"), None),
        P("leaf", None, "col"),
        P("leaf", None, None),
        P("leaf", None, None, None),
        P("leaf", None, None),
        P("leaf", None, None, None),
    )
    return jax.shard_map(
        on_device,
        mesh=mesh,
        in_specs=placed,
        out_specs=(P("leaf", None, "col"), P("leaf", None, "col")),
        check_vma=False,
    )
```

```python
import functools

import jax
import jax.numpy as jnp
from jax import lax
from jax.experimental import pallas as pl
from jax.experimental.pallas import tpu as pltpu
from jax.sharding import PartitionSpec as P

F32 = jnp.float32
BF16 = jnp.bfloat16
FORWARD_VMEM = 60 * 2**20
LEAF_VMEM = 10 * 2**20
TREE_VMEM = 6 * 2**20
BATCH = 4
PART = 3


def swap(value, axis, mask):
    pairs = [(source, source ^ mask) for source in range(lax.axis_size(axis))]
    return lax.ppermute(value, axis, pairs)


def dot(left, right):
    return jnp.dot(left, right, preferred_element_type=F32)


def cost(flops, moved):
    return pl.CostEstimate(flops=flops, bytes_accessed=moved, transcendentals=0)


def forward_kernel(first, last, scalars, ancestors, rhs, far, inv, panels, start, *refs):
    if last:
        value, own_total, far_total, solved, held, sems = refs
    else:
        value, total, solved, held, sems = refs
    step, steps = pl.program_id(0), pl.num_programs(0)
    batch, slots = panels.shape[:2]
    levels, _, both = held.shape
    cols = both // 2

    def leaving(leaf):
        return pltpu.make_async_copy(solved.at[leaf], value.at[leaf], sems.at[leaf])

    @pl.when(step == 0)
    def _():
        if first:
            for level in range(levels):
                held[level, :, :cols] = start[0].astype(F32) * -(scalars[2] == level + 1).astype(F32)
                held[level, :, cols:] = jnp.zeros((held.shape[1], cols), F32)
        else:
            held[...] = start[...]

    values = []
    for leaf in range(batch):
        columns = jnp.concatenate([rhs[leaf], far[leaf]], axis=1)
        values.append(dot(inv[leaf], columns).astype(BF16))
        solved[step * batch + leaf] = values[leaf]
        leaving(step * batch + leaf).start()
    sums = [None] * levels
    for leaf in range(batch):
        for slot in range(slots):
            product = dot(panels[leaf, slot], values[leaf])
            named = ancestors[step * batch + leaf, slot]
            for level in range(levels):
                term = product * (named == level + 1).astype(F32)
                sums[level] = term if sums[level] is None else sums[level] + term
    for level in range(levels):
        held[level] += sums[level]

    @pl.when(step == steps - 1)
    def _():
        if last:
            own_total[...] = held[:, :, :cols].astype(BF16)
            far_total[...] = held[:, :, cols:].astype(BF16)
        else:
            total[...] = held[...]
        for leaf in range(solved.shape[0]):
            leaving(leaf).wait()


def forward(levels, scalars, which, ancestors, inv, panels, rhs, far, start, first, last):
    count, size, _ = inv.shape
    cols = rhs.shape[2]
    slots = panels.shape[1]
    batch = min(BATCH, count)
    whole = lambda i, *_: (0, 0, 0)
    if last:
        sums = [jax.ShapeDtypeStruct((levels, size, cols), BF16)] * 2
    else:
        sums = [jax.ShapeDtypeStruct((levels, size, 2 * cols), F32)]
    return pl.pallas_call(
        functools.partial(forward_kernel, first, last),
        grid_spec=pltpu.PrefetchScalarGridSpec(
            num_scalar_prefetch=2,
            grid=(count // batch,),
            in_specs=[
                pl.BlockSpec((batch, size, cols), lambda i, scalars, _: (scalars[which] // batch + i, 0, 0)),
                pl.BlockSpec((batch, size, cols), lambda i, *_: (i, 0, 0)),
                pl.BlockSpec((batch, size, size), lambda i, *_: (i, 0, 0)),
                pl.BlockSpec((batch, slots, size, size), lambda i, *_: (i, 0, 0, 0)),
                pl.BlockSpec(start.shape, whole),
            ],
            out_specs=[pl.BlockSpec(memory_space=pl.ANY)] + [pl.BlockSpec(part.shape, whole) for part in sums],
            scratch_shapes=[
                pltpu.VMEM((count, size, 2 * cols), BF16),
                pltpu.VMEM((levels, size, 2 * cols), F32),
                pltpu.SemaphoreType.DMA((count,)),
            ],
        ),
        out_shape=[jax.ShapeDtypeStruct((count, size, 2 * cols), BF16)] + sums,
        compiler_params=pltpu.CompilerParams(vmem_limit_bytes=FORWARD_VMEM),
        cost_estimate=cost(0, 0),
        name="leaf_forward",
    )(scalars, ancestors, rhs, far, inv, panels, start)


def solve_leaves(base, step, batch, ancestors, value, inv, panels, paths):
    leaves = [step * batch + index for index in range(batch)]
    rests = []
    for leaf in leaves:
        update = None
        for slot in range(panels.shape[1]):
            level = ancestors[base + leaf, slot]
            picked = paths[jnp.maximum(level - 1, 0)]
            picked = jnp.where(level > 0, picked, jnp.zeros_like(picked))
            term = dot(panels[leaf, slot], picked)
            update = term if update is None else update + term
        rests.append((value[leaf].astype(F32) - update).astype(BF16))
    return [dot(inv[leaf], rest).astype(BF16) for leaf, rest in zip(leaves, rests)]


def send_kernel(base, ancestors, value, inv, panels, paths, result):
    step = pl.program_id(0)
    batch = result.shape[0]
    solutions = solve_leaves(base + step * batch, 0, batch, ancestors, value, inv, panels, paths)
    for index, solution_block in enumerate(solutions):
        result[index] = solution_block


def solve_far(ancestors, inv, panels, value, paths, base, count):
    levels, size, cols = paths.shape[0], paths.shape[1], paths.shape[2] // 2
    batch = min(BATCH, count)
    ahead = base // batch

    def part(array):
        block = (batch,) + array.shape[1:]
        return pl.BlockSpec(block, lambda i: (ahead + i,) + (0,) * (array.ndim - 1))

    return pl.pallas_call(
        functools.partial(send_kernel, base),
        grid=(count // batch,),
        in_specs=[
            pl.BlockSpec(memory_space=pltpu.SMEM),
            pl.BlockSpec((batch, size, cols), lambda i: (ahead + i, 0, 1)),
            part(inv),
            part(panels),
            pl.BlockSpec((levels, size, cols), lambda i: (0, 0, 1)),
        ],
        out_specs=pl.BlockSpec((batch, size, cols), lambda i: (i, 0, 0)),
        out_shape=jax.ShapeDtypeStruct((count, size, cols), BF16),
        compiler_params=pltpu.CompilerParams(vmem_limit_bytes=LEAF_VMEM),
        cost_estimate=cost(0, 0),
        name="solve_far",
    )(ancestors, value, inv, panels, paths)


def keep_kernel(which, scalars, ancestors, value, inv, panels, paths, *refs):
    result, solved, sems = refs[-3:]
    step, steps = pl.program_id(0), pl.num_programs(0)
    batch = value.shape[0]

    def leaving(leaf):
        return pltpu.make_async_copy(solved.at[leaf], result.at[scalars[which] + leaf], sems.at[leaf])

    for index, solution_block in enumerate(solve_leaves(step * batch, 0, batch, ancestors, value, inv, panels, paths)):
        solved[step * batch + index] = solution_block
        leaving(step * batch + index).start()

    @pl.when(step == steps - 1)
    def _():
        for leaf in range(solved.shape[0]):
            leaving(leaf).wait()


def solve_own(scalars, which, ancestors, inv, panels, value, paths, rows, into=None):
    levels, size, cols = paths.shape[0], paths.shape[1], paths.shape[2] // 2
    count, slots = panels.shape[:2]
    batch = min(BATCH, count)
    extra = [] if into is None else [into]
    hbm, smem = pl.BlockSpec(memory_space=pl.ANY), pl.BlockSpec(memory_space=pltpu.SMEM)
    return pl.pallas_call(
        functools.partial(keep_kernel, which),
        grid=(count // batch,),
        in_specs=[
            smem,
            smem,
            pl.BlockSpec((batch, size, cols), lambda i: (i, 0, 0)),
            pl.BlockSpec((batch, size, size), lambda i: (i, 0, 0)),
            pl.BlockSpec((batch, slots, size, size), lambda i: (i, 0, 0, 0)),
            pl.BlockSpec((levels, size, cols), lambda i: (0, 0, 0)),
        ]
        + [hbm] * len(extra),
        out_specs=hbm,
        out_shape=jax.ShapeDtypeStruct((rows, size, cols), BF16),
        scratch_shapes=[pltpu.VMEM((count, size, cols), BF16), pltpu.SemaphoreType.DMA((count,))],
        input_output_aliases={} if into is None else {6: 0},
        compiler_params=pltpu.CompilerParams(vmem_limit_bytes=LEAF_VMEM),
        cost_estimate=cost(0, 0),
        name="solve_own",
    )(scalars, ancestors, value, inv, panels, paths, *extra)


def place_kernel(scalars, part, whole, result):
    result[...] = part[...]


def place_rows(scalars, which, offset, part, whole):
    count, size, cols = part.shape
    return pl.pallas_call(
        place_kernel,
        grid_spec=pltpu.PrefetchScalarGridSpec(
            num_scalar_prefetch=1,
            grid=(1,),
            in_specs=[pl.BlockSpec(part.shape, lambda i, _: (0, 0, 0)), pl.BlockSpec(memory_space=pl.ANY)],
            out_specs=pl.BlockSpec(part.shape, lambda i, scalars: ((scalars[which] + offset) // count, 0, 0)),
        ),
        out_shape=jax.ShapeDtypeStruct(whole.shape, whole.dtype),
        input_output_aliases={2: 0},
        compiler_params=pltpu.CompilerParams(vmem_limit_bytes=LEAF_VMEM),
        cost_estimate=cost(0, 0),
        name="place_rows",
    )(scalars, part, whole)


def combine_kernel(lower_inv, lower_panels, upper_inv, upper_panels, blocks, *parts):
    made = [dot(upper_inv[0], lower_inv[0]).astype(BF16)]
    for slot in range(blocks.shape[0] // 2):
        made.append(dot(lower_panels[0, slot], lower_inv[0]).astype(BF16))
        made.append(dot(upper_inv[0], upper_panels[0, slot]).astype(BF16))
    for index, block in enumerate(made):
        blocks[index] = block
    for part in parts:
        for index in range(part.shape[0]):
            part[index] = made.pop(0)


def combine(lower_inv, lower_panels, upper_inv, upper_panels):
    size = lower_inv.shape[1]
    total = 1 + 2 * lower_panels.shape[1]
    counts = [total] + [min(PART, total - begin) for begin in range(0, total, PART)]
    blocks, *parts = pl.pallas_call(
        combine_kernel,
        out_shape=[jax.ShapeDtypeStruct((blocks, size, size), BF16) for blocks in counts],
        compiler_params=pltpu.CompilerParams(vmem_limit_bytes=TREE_VMEM),
        cost_estimate=cost(2**20, 2**20),
        name="combine",
    )(lower_inv, lower_panels, upper_inv, upper_panels)
    return blocks, parts


def sort_kernel(parts, wanted, flags, mine, *refs):
    theirs, chosen = refs[:parts], refs[parts:]

    @pl.when(flags[0] == wanted)
    def _():
        for out in chosen:
            out[...] = mine[: out.shape[0]]

    @pl.when(flags[0] != wanted)
    def _():
        for out in chosen:
            begin = 0
            for part in theirs:
                for index in range(min(part.shape[0], out.shape[0] - begin)):
                    out[begin + index] = part[index]
                begin += part.shape[0]


def sort(bit, wanted, mine, theirs, counts):
    memory = pl.BlockSpec(memory_space=pltpu.VMEM)
    return pl.pallas_call(
        functools.partial(sort_kernel, len(theirs), wanted),
        in_specs=[pl.BlockSpec(memory_space=pltpu.SMEM), memory] + [memory] * len(theirs),
        out_specs=[memory] * len(counts),
        out_shape=[jax.ShapeDtypeStruct((count,) + mine.shape[1:], BF16) for count in counts],
        compiler_params=pltpu.CompilerParams(vmem_limit_bytes=TREE_VMEM),
        cost_estimate=cost(2**20, 2**20),
        name="sort",
    )(jnp.reshape(bit, (1,)).astype(jnp.int32), mine, *theirs)


def pick_kernel(flags, *refs):
    sources, chosen, sem = refs[:-2], refs[-2], refs[-1]
    for index, source in enumerate(sources):

        @pl.when(flags[0] == index)
        def _(source=source):
            copy = pltpu.make_async_copy(source.at[:1], chosen, sem)
            copy.start()
            copy.wait()


def pick(index, sources):
    return pl.pallas_call(
        pick_kernel,
        in_specs=[pl.BlockSpec(memory_space=pltpu.SMEM)] + [pl.BlockSpec(memory_space=pl.ANY)] * len(sources),
        out_specs=pl.BlockSpec(memory_space=pltpu.VMEM),
        out_shape=jax.ShapeDtypeStruct((1,) + sources[0].shape[1:], BF16),
        scratch_shapes=[pltpu.SemaphoreType.DMA],
        compiler_params=pltpu.CompilerParams(vmem_limit_bytes=TREE_VMEM),
        cost_estimate=cost(2**20, 2**20),
        name="pick",
    )(jnp.reshape(index, (1,)).astype(jnp.int32), *sources)


def from_owners(value, level, hop):
    owner = 2 ** (level - 1)
    pairs = [
        (group + owner + index, group + (owner + index ^ hop))
        for group in range(0, lax.axis_size("leaf"), 2**level)
        for index in range(2)
    ]
    return lax.ppermute(value, "leaf", pairs)


def after(value, *earlier):
    return lax.optimization_barrier((value, *earlier))[0]


def climb_kernel(mine, theirs, factors, passed, entered, *both):
    here = (-(mine[0].astype(F32) + theirs[0].astype(F32))).astype(BF16)
    for above in range(passed.shape[0]):
        carried = mine[above + 1].astype(F32) + theirs[above + 1].astype(F32)
        passed[above] = (carried + dot(factors[1 + 2 * above], here)).astype(BF16)
    entered[0] = here
    if passed.shape[0] == 1:
        entered[1] = passed[0]


def climb(mine, theirs, factors):
    levels, size, cols = mine.shape
    vmem = pl.BlockSpec(memory_space=pltpu.VMEM)
    return pl.pallas_call(
        climb_kernel,
        in_specs=[vmem] * 3,
        out_specs=[vmem] * 2,
        out_shape=[
            jax.ShapeDtypeStruct((levels - 1, size, cols), BF16),
            jax.ShapeDtypeStruct((2 if levels == 2 else 1, size, cols), BF16),
        ],
        compiler_params=pltpu.CompilerParams(vmem_limit_bytes=TREE_VMEM),
        cost_estimate=cost(2**20, 2**20),
        name="climb",
    )(mine, theirs, factors)


def hold_kernel(below, factors, next_factors, *refs):
    refs, (kept, inputs, onward) = refs[:-3], refs[-3:]
    begin = 0
    if below == 1:
        begin = refs[0].shape[0]
        kept[:begin] = refs[0][...]
        cols = refs[2].shape[2]
        if inputs.shape[0] > 1:
            inputs[:-1] = refs[1][...]
        inputs[inputs.shape[0] - 1, :, :cols] = refs[2][0]
        inputs[inputs.shape[0] - 1, :, cols:] = refs[3][0]
    else:
        inputs[...] = jnp.zeros(inputs.shape, BF16)
    count = factors.shape[0] // 2
    for above in range(count):
        kept[begin + above] = factors[2 + 2 * above]
    kept[begin + count] = factors[0]
    onward[...] = next_factors[...]


def hold(level, factors, next_factors, before):
    size = factors.shape[1]
    vmem = pl.BlockSpec(memory_space=pltpu.VMEM)
    blocks = factors.shape[0] // 2 + 1 + (before[0].shape[0] if before else 0)
    cols = 2 * before[2].shape[2] if before else size
    *held, onward = pl.pallas_call(
        functools.partial(hold_kernel, len(before) // 4),
        in_specs=[vmem] * (2 + len(before)),
        out_specs=[vmem] * 3,
        out_shape=[
            jax.ShapeDtypeStruct((blocks, size, size), BF16),
            jax.ShapeDtypeStruct((max(level - 1, 1), size, cols), BF16),
            jax.ShapeDtypeStruct(next_factors.shape, BF16),
        ],
        compiler_params=pltpu.CompilerParams(vmem_limit_bytes=TREE_VMEM),
        cost_estimate=cost(2**20, 2**20),
        name="hold",
    )(factors, next_factors, *before)
    return held, onward


def descend_kernel(own, far, theirs, across, top, kept, inputs, paths):
    levels = paths.shape[0]
    entered = [own[1].astype(F32) + theirs[0].astype(F32), far[1].astype(F32) + across[0].astype(F32)]
    entered = (-jnp.concatenate(entered, axis=1)).astype(BF16)
    paths[levels - 1] = dot(top[0], entered).astype(BF16)
    end = kept.shape[0]
    for level in range(levels - 2, -1, -1):
        count = levels - 1 - level
        end -= count + 1
        if level == levels - 2:
            entered = jnp.concatenate([own[0], far[0]], axis=1)
        else:
            entered = inputs[level]
        rest = dot(kept[end + count], entered)
        for above in reversed(range(count)):
            rest = rest - dot(kept[end + above], paths[level + 1 + above])
        paths[level] = rest.astype(BF16)


def descend(levels, own, far, theirs, across, top, kept, inputs):
    _, size, cols = own.shape
    vmem = pl.BlockSpec(memory_space=pltpu.VMEM)
    return pl.pallas_call(
        descend_kernel,
        in_specs=[vmem] * 7,
        out_specs=vmem,
        out_shape=jax.ShapeDtypeStruct((levels, size, 2 * cols), BF16),
        compiler_params=pltpu.CompilerParams(vmem_limit_bytes=TREE_VMEM),
        cost_estimate=cost(2**20, 2**20),
        name="descend",
    )(own, far, theirs, across, top, kept, inputs)


def on_device(
    leaf_rhs,
    leaf_lower_inv,
    leaf_lower_panels,
    leaf_upper_inv,
    leaf_upper_panels,
    ancestors,
    sep_rhs,
    sep_lower_inv,
    sep_lower_panels,
    sep_upper_inv,
    sep_upper_panels,
):
    levels = lax.axis_size("leaf").bit_length() - 1
    device = lax.axis_index("leaf")
    place = lax.axis_index("col")
    low, high = place % 2, place // 2
    count = leaf_lower_inv.shape[0]
    rows, size, cols = leaf_rhs.shape

    first = high * 2 * count + low * count
    second = high * 2 * count + (1 - low) * count
    owned = [device % 2**level == 2 ** (level - 1) for level in range(1, levels + 1)]
    own_level = sum(jnp.where(is_owner, level, 0) for level, is_owner in enumerate(owned, 1))

    away = (1 - high) * 2 * count
    scalars = jnp.stack([first, second, own_level, away + low * count, away + (1 - low) * count]).astype(jnp.int32)
    half = count // 2
    sent = [lax.dynamic_slice_in_dim(leaf_rhs, away + low * count, count, 0)]
    sent.append(lax.dynamic_slice_in_dim(after(leaf_rhs, sent[0]), away + (1 - low) * count, count, 0))
    far_rhs = [swap(part, "col", 2) for part in sent]

    near_ancestors = swap(ancestors, "col", 1)
    near_lower_inv = swap(leaf_lower_inv, "col", 1)
    near_lower_panels = swap(leaf_lower_panels, "col", 1)
    local = (ancestors, leaf_lower_inv, leaf_lower_panels)
    near = (near_ancestors, near_lower_inv, near_lower_panels)

    blocks, pieces = combine(after(sep_lower_inv, *sent), sep_lower_panels, sep_upper_inv, sep_upper_panels)

    start = after(sep_rhs, *near)
    value_1, total = forward(levels, scalars, 0, *local, leaf_rhs, far_rhs[0], start, True, False)
    arrived = [swap(piece, "leaf", 1) for piece in pieces]
    count_above = blocks.shape[0] - 2
    onward = sort(device % 2, 0, blocks, after(arrived, total), (count_above, 1)) if levels > 1 else []
    total = after(total, *onward)
    value_2, own_total, far_total = forward(levels, scalars, 1, *near, leaf_rhs, far_rhs[1], total, False, True)

    if levels == 3:
        from_top = [from_owners(onward[1], levels, hop) for hop in (4, 6)]
        far_total = after(far_total, *from_top)
    mine = (own_total.astype(F32) + swap(far_total, "col", 2).astype(F32)).astype(BF16)
    if levels == 3:
        from_top = pick(device // 2 % 2, from_top)
        mine = after(mine, from_top)
    (factors,) = sort(device % 2, 1, blocks, after(arrived, mine), (blocks.shape[0],))
    held = []
    for level in range(1, levels):
        theirs = swap(mine, "leaf", 2 ** (level - 1))
        here = onward[0]
        if levels != 3 or level == 1:
            arrived = swap(here, "leaf", 2**level)
            (following,) = sort(device // 2**level % 2, 1, here, [arrived], (here.shape[0],))
        if level < levels - 1 and levels != 3:
            onward = sort(device // 2**level % 2, 0, here, [arrived], (here.shape[0] - 2, 1))
        if levels == 3 and level == 1:
            (candidate,) = sort(device // 2 % 2, 0, here, [arrived], (1,))
            theirs = after(theirs, following, candidate)
            top = pick(device // 4 % 2, [from_top, candidate])
        elif levels == 3:
            following = top
            theirs = after(theirs, top)
        else:
            theirs = after(theirs, following)
        passed, entered = climb(mine, theirs, factors)
        if level == 1:
            near_upper_inv = swap(after(leaf_upper_inv, passed), "col", 1)
            near_upper_panels = swap(after(leaf_upper_panels, passed), "col", 1)
        held, following = hold(level, after(factors, passed), following, [*held, own, far] if level > 1 else [])
        mine, factors, own, far = passed, following, entered, swap(entered, "col", 2)
    theirs = swap(mine, "leaf", 2 ** (levels - 1))
    hop = 2 ** (levels - 1) * lax.axis_size("col") + 2
    pairs = [(source, source ^ hop) for source in range(lax.axis_size("leaf") * lax.axis_size("col"))]
    across = lax.ppermute(mine, ("leaf", "col"), pairs)
    paths = descend(levels, own, far, theirs, across, factors, *held)

    own_solution = jnp.zeros((size, cols), BF16)
    for level in range(levels):
        own_solution = jnp.where(owned[level], paths[level, :, :cols], own_solution)

    local = (ancestors, leaf_upper_inv, leaf_upper_panels)
    near = (near_ancestors, near_upper_inv, near_upper_panels)
    leaf_solution = solve_own(scalars, 0, *local, value_1, paths, rows)
    returning = [
        (3, 0, solve_far(*local, value_1, paths, 0, count)),
        (4, 0, solve_far(*near, value_2, paths, 0, half)),
        (4, half, solve_far(*near, value_2, paths, half, half)),
    ]
    leaf_solution = solve_own(scalars, 1, *near, value_2, paths, rows, leaf_solution)
    for which, offset, part in returning:
        leaf_solution = place_rows(scalars, which, offset, swap(part, "col", 2), leaf_solution)
    return (leaf_solution, own_solution[None])


def solution(mesh):
    placed = (
        P("leaf", None, "col"),
        P(("leaf", "col"), None, None),
        P(("leaf", "col"), None, None, None),
        P(("leaf", "col"), None, None),
        P(("leaf", "col"), None, None, None),
        P(("leaf", "col"), None),
        P("leaf", None, "col"),
        P("leaf", None, None),
        P("leaf", None, None, None),
        P("leaf", None, None),
        P("leaf", None, None, None),
    )
    return jax.shard_map(
        on_device,
        mesh=mesh,
        in_specs=placed,
        out_specs=(P("leaf", None, "col"), P("leaf", None, "col")),
        check_vma=False,
    )
```

```python
import functools

import jax
import jax.numpy as jnp
from jax import lax
from jax.experimental import pallas as pl
from jax.experimental.pallas import tpu as pltpu
from jax.sharding import PartitionSpec as P

F32 = jnp.float32
BF16 = jnp.bfloat16
FORWARD_VMEM = 60 * 2**20
LEAF_VMEM = 10 * 2**20
TREE_VMEM = 6 * 2**20
BATCH = 4
PART = 3


def swap(value, axis, mask):
    pairs = [(source, source ^ mask) for source in range(lax.axis_size(axis))]
    return lax.ppermute(value, axis, pairs)


def dot(left, right):
    return jnp.dot(left, right, preferred_element_type=F32)


def cost(flops, moved):
    return pl.CostEstimate(flops=flops, bytes_accessed=moved, transcendentals=0)


def forward_kernel(own, far, first, scalars, ancestors, *refs):
    sides = own + far
    columns_in, (inv, panels, start) = refs[:sides], refs[sides : sides + 3]
    value, *totals = refs[sides + 3 : -3]
    solved, held, sems = refs[-3:]
    step, steps = pl.program_id(0), pl.num_programs(0)
    batch, slots = panels.shape[:2]
    levels = held.shape[0]
    cols = start.shape[2]

    def leaving(leaf):
        return pltpu.make_async_copy(solved.at[leaf], value.at[leaf], sems.at[leaf])

    @pl.when(step == 0)
    def _():
        if first:
            for level in range(levels):
                held[level] = start[0].astype(F32) * -(scalars[2] == level + 1).astype(F32)
        else:
            held[:, :, :cols] = start[...]
            if sides == 2:
                held[:, :, cols:] = jnp.zeros((levels, held.shape[1], cols), F32)

    values = []
    for leaf in range(batch):
        columns = [array[leaf] for array in columns_in]
        columns = jnp.concatenate(columns, axis=1) if sides == 2 else columns[0]
        values.append(dot(inv[leaf], columns).astype(BF16))
        solved[step * batch + leaf] = values[leaf]
        leaving(step * batch + leaf).start()
    sums = [None] * levels
    for leaf in range(batch):
        for slot in range(slots):
            product = dot(panels[leaf, slot], values[leaf])
            named = ancestors[step * batch + leaf, slot]
            for level in range(levels):
                term = product * (named == level + 1).astype(F32)
                sums[level] = term if sums[level] is None else sums[level] + term
    for level in range(levels):
        held[level] += sums[level]

    @pl.when(step == steps - 1)
    def _():
        for side, total in enumerate(totals):
            total[...] = held[:, :, side * cols : (side + 1) * cols].astype(total.dtype)
        for leaf in range(solved.shape[0]):
            leaving(leaf).wait()


def forward(levels, scalars, which, ancestors, inv, panels, rhs, far, start, first, types):
    count, size, _ = inv.shape
    cols = start.shape[2]
    slots = panels.shape[1]
    batch = min(BATCH, count)
    whole = lambda i, *_: (0, 0, 0)
    sides = [array for array in (rhs, far) if array is not None]
    specs = []
    if rhs is not None:
        specs.append(pl.BlockSpec((batch, size, cols), lambda i, scalars, _: (scalars[which] // batch + i, 0, 0)))
    if far is not None:
        specs.append(pl.BlockSpec((batch, size, cols), lambda i, *_: (i, 0, 0)))
    sums = [jax.ShapeDtypeStruct((levels, size, cols), kind) for kind in types]
    return pl.pallas_call(
        functools.partial(forward_kernel, rhs is not None, far is not None, first),
        grid_spec=pltpu.PrefetchScalarGridSpec(
            num_scalar_prefetch=2,
            grid=(count // batch,),
            in_specs=specs
            + [
                pl.BlockSpec((batch, size, size), lambda i, *_: (i, 0, 0)),
                pl.BlockSpec((batch, slots, size, size), lambda i, *_: (i, 0, 0, 0)),
                pl.BlockSpec(start.shape, whole),
            ],
            out_specs=[pl.BlockSpec(memory_space=pl.ANY)] + [pl.BlockSpec(part.shape, whole) for part in sums],
            scratch_shapes=[
                pltpu.VMEM((count, size, len(sides) * cols), BF16),
                pltpu.VMEM((levels, size, len(sides) * cols), F32),
                pltpu.SemaphoreType.DMA((count,)),
            ],
        ),
        out_shape=[jax.ShapeDtypeStruct((count, size, len(sides) * cols), BF16)] + sums,
        compiler_params=pltpu.CompilerParams(vmem_limit_bytes=FORWARD_VMEM),
        cost_estimate=cost(0, 0),
        name="leaf_forward",
    )(scalars, ancestors, *sides, inv, panels, start)


def solve_leaves(base, step, batch, ancestors, value, inv, panels, paths):
    leaves = [step * batch + index for index in range(batch)]
    rests = []
    for leaf in leaves:
        update = None
        for slot in range(panels.shape[1]):
            level = ancestors[base + leaf, slot]
            picked = paths[jnp.maximum(level - 1, 0)]
            picked = jnp.where(level > 0, picked, jnp.zeros_like(picked))
            term = dot(panels[leaf, slot], picked)
            update = term if update is None else update + term
        rests.append((value[leaf].astype(F32) - update).astype(BF16))
    return [dot(inv[leaf], rest).astype(BF16) for leaf, rest in zip(leaves, rests)]


def send_kernel(base, ancestors, value, inv, panels, paths, result):
    step = pl.program_id(0)
    batch = result.shape[0]
    solutions = solve_leaves(base + step * batch, 0, batch, ancestors, value, inv, panels, paths)
    for index, solution_block in enumerate(solutions):
        result[index] = solution_block


def solve_far(ancestors, inv, panels, value, paths, base, count):
    levels, size, cols = paths.shape[0], paths.shape[1], paths.shape[2] // 2
    batch = max(leaves for leaves in range(1, BATCH + 1) if count % leaves == 0 and base % leaves == 0)
    ahead = base // batch

    def part(array):
        block = (batch,) + array.shape[1:]
        return pl.BlockSpec(block, lambda i: (ahead + i,) + (0,) * (array.ndim - 1))

    return pl.pallas_call(
        functools.partial(send_kernel, base),
        grid=(count // batch,),
        in_specs=[
            pl.BlockSpec(memory_space=pltpu.SMEM),
            pl.BlockSpec((batch, size, cols), lambda i: (ahead + i, 0, value.shape[2] // cols - 1)),
            part(inv),
            part(panels),
            pl.BlockSpec((levels, size, cols), lambda i: (0, 0, 1)),
        ],
        out_specs=pl.BlockSpec((batch, size, cols), lambda i: (i, 0, 0)),
        out_shape=jax.ShapeDtypeStruct((count, size, cols), BF16),
        compiler_params=pltpu.CompilerParams(vmem_limit_bytes=LEAF_VMEM),
        cost_estimate=cost(0, 0),
        name="solve_far",
    )(ancestors, value, inv, panels, paths)


def keep_kernel(which, scalars, ancestors, value, inv, panels, paths, *refs):
    result, solved, sems = refs[-3:]
    step, steps = pl.program_id(0), pl.num_programs(0)
    batch = value.shape[0]

    def leaving(leaf):
        return pltpu.make_async_copy(solved.at[leaf], result.at[scalars[which] + leaf], sems.at[leaf])

    for index, solution_block in enumerate(solve_leaves(step * batch, 0, batch, ancestors, value, inv, panels, paths)):
        solved[step * batch + index] = solution_block
        leaving(step * batch + index).start()

    @pl.when(step == steps - 1)
    def _():
        for leaf in range(solved.shape[0]):
            leaving(leaf).wait()


def solve_own(scalars, which, ancestors, inv, panels, value, paths, rows, into=None):
    levels, size, cols = paths.shape[0], paths.shape[1], paths.shape[2] // 2
    count, slots = panels.shape[:2]
    batch = min(BATCH, count)
    extra = [] if into is None else [into]
    hbm, smem = pl.BlockSpec(memory_space=pl.ANY), pl.BlockSpec(memory_space=pltpu.SMEM)
    return pl.pallas_call(
        functools.partial(keep_kernel, which),
        grid=(count // batch,),
        in_specs=[
            smem,
            smem,
            pl.BlockSpec((batch, size, cols), lambda i: (i, 0, 0)),
            pl.BlockSpec((batch, size, size), lambda i: (i, 0, 0)),
            pl.BlockSpec((batch, slots, size, size), lambda i: (i, 0, 0, 0)),
            pl.BlockSpec((levels, size, cols), lambda i: (0, 0, 0)),
        ]
        + [hbm] * len(extra),
        out_specs=hbm,
        out_shape=jax.ShapeDtypeStruct((rows, size, cols), BF16),
        scratch_shapes=[pltpu.VMEM((count, size, cols), BF16), pltpu.SemaphoreType.DMA((count,))],
        input_output_aliases={} if into is None else {6: 0},
        compiler_params=pltpu.CompilerParams(vmem_limit_bytes=LEAF_VMEM),
        cost_estimate=cost(0, 0),
        name="solve_own",
    )(scalars, ancestors, value, inv, panels, paths, *extra)


def place_kernel(scalars, part, whole, result):
    result[...] = part[...]


def place_rows(scalars, which, offset, part, whole):
    count, size, cols = part.shape
    batch = max(leaves for leaves in (8, 4, 2, 1) if count % leaves == 0 and offset % leaves == 0)
    return pl.pallas_call(
        place_kernel,
        grid_spec=pltpu.PrefetchScalarGridSpec(
            num_scalar_prefetch=1,
            grid=(count // batch,),
            in_specs=[
                pl.BlockSpec((batch, size, cols), lambda i, _: (i, 0, 0)),
                pl.BlockSpec(memory_space=pl.ANY),
            ],
            out_specs=pl.BlockSpec(
                (batch, size, cols), lambda i, scalars: ((scalars[which] + offset) // batch + i, 0, 0)
            ),
        ),
        out_shape=jax.ShapeDtypeStruct(whole.shape, whole.dtype),
        input_output_aliases={2: 0},
        compiler_params=pltpu.CompilerParams(vmem_limit_bytes=LEAF_VMEM),
        cost_estimate=cost(0, 0),
        name="place_rows",
    )(scalars, part, whole)


def combine_kernel(lower_inv, lower_panels, upper_inv, upper_panels, blocks, *parts):
    made = [dot(upper_inv[0], lower_inv[0]).astype(BF16)]
    for slot in range(blocks.shape[0] // 2):
        made.append(dot(lower_panels[0, slot], lower_inv[0]).astype(BF16))
        made.append(dot(upper_inv[0], upper_panels[0, slot]).astype(BF16))
    for index, block in enumerate(made):
        blocks[index] = block
    for part in parts:
        for index in range(part.shape[0]):
            part[index] = made.pop(0)


def combine(lower_inv, lower_panels, upper_inv, upper_panels):
    size = lower_inv.shape[1]
    total = 1 + 2 * lower_panels.shape[1]
    counts = [total] + [min(PART, total - begin) for begin in range(0, total, PART)]
    blocks, *parts = pl.pallas_call(
        combine_kernel,
        out_shape=[jax.ShapeDtypeStruct((blocks, size, size), BF16) for blocks in counts],
        compiler_params=pltpu.CompilerParams(vmem_limit_bytes=TREE_VMEM),
        cost_estimate=cost(2**20, 2**20),
        name="combine",
    )(lower_inv, lower_panels, upper_inv, upper_panels)
    return blocks, parts


def sort_kernel(parts, wanted, flags, mine, *refs):
    theirs, chosen = refs[:parts], refs[parts:]

    @pl.when(flags[0] == wanted)
    def _():
        for out in chosen:
            out[...] = mine[: out.shape[0]]

    @pl.when(flags[0] != wanted)
    def _():
        for out in chosen:
            begin = 0
            for part in theirs:
                for index in range(min(part.shape[0], out.shape[0] - begin)):
                    out[begin + index] = part[index]
                begin += part.shape[0]


def sort(bit, wanted, mine, theirs, counts):
    memory = pl.BlockSpec(memory_space=pltpu.VMEM)
    return pl.pallas_call(
        functools.partial(sort_kernel, len(theirs), wanted),
        in_specs=[pl.BlockSpec(memory_space=pltpu.SMEM), memory] + [memory] * len(theirs),
        out_specs=[memory] * len(counts),
        out_shape=[jax.ShapeDtypeStruct((count,) + mine.shape[1:], BF16) for count in counts],
        compiler_params=pltpu.CompilerParams(vmem_limit_bytes=TREE_VMEM),
        cost_estimate=cost(2**20, 2**20),
        name="sort",
    )(jnp.reshape(bit, (1,)).astype(jnp.int32), mine, *theirs)


def pick_kernel(flags, *refs):
    sources, chosen, sem = refs[:-2], refs[-2], refs[-1]
    for index, source in enumerate(sources):

        @pl.when(flags[0] == index)
        def _(source=source):
            copy = pltpu.make_async_copy(source.at[:1], chosen, sem)
            copy.start()
            copy.wait()


def pick(index, sources):
    return pl.pallas_call(
        pick_kernel,
        in_specs=[pl.BlockSpec(memory_space=pltpu.SMEM)] + [pl.BlockSpec(memory_space=pl.ANY)] * len(sources),
        out_specs=pl.BlockSpec(memory_space=pltpu.VMEM),
        out_shape=jax.ShapeDtypeStruct((1,) + sources[0].shape[1:], BF16),
        scratch_shapes=[pltpu.SemaphoreType.DMA],
        compiler_params=pltpu.CompilerParams(vmem_limit_bytes=TREE_VMEM),
        cost_estimate=cost(2**20, 2**20),
        name="pick",
    )(jnp.reshape(index, (1,)).astype(jnp.int32), *sources)


def from_owners(value, level, hop):
    owner = 2 ** (level - 1)
    pairs = [
        (group + owner + index, group + (owner + index ^ hop))
        for group in range(0, lax.axis_size("leaf"), 2**level)
        for index in range(2)
    ]
    return lax.ppermute(value, "leaf", pairs)


def after(value, *earlier):
    return lax.optimization_barrier((value, *earlier))[0]


def climb_kernel(mine, theirs, factors, passed, entered, *both):
    here = (-(mine[0].astype(F32) + theirs[0].astype(F32))).astype(BF16)
    for above in range(passed.shape[0]):
        carried = mine[above + 1].astype(F32) + theirs[above + 1].astype(F32)
        passed[above] = (carried + dot(factors[1 + 2 * above], here)).astype(BF16)
    entered[0] = here
    if passed.shape[0] == 1:
        entered[1] = passed[0]


def climb(mine, theirs, factors):
    levels, size, cols = mine.shape
    vmem = pl.BlockSpec(memory_space=pltpu.VMEM)
    return pl.pallas_call(
        climb_kernel,
        in_specs=[vmem] * 3,
        out_specs=[vmem] * 2,
        out_shape=[
            jax.ShapeDtypeStruct((levels - 1, size, cols), BF16),
            jax.ShapeDtypeStruct((2 if levels == 2 else 1, size, cols), BF16),
        ],
        compiler_params=pltpu.CompilerParams(vmem_limit_bytes=TREE_VMEM),
        cost_estimate=cost(2**20, 2**20),
        name="climb",
    )(mine, theirs, factors)


def hold_kernel(below, factors, next_factors, *refs):
    refs, (kept, inputs, onward) = refs[:-3], refs[-3:]
    begin = 0
    if below == 1:
        begin = refs[0].shape[0]
        kept[:begin] = refs[0][...]
        cols = refs[2].shape[2]
        if inputs.shape[0] > 1:
            inputs[:-1] = refs[1][...]
        inputs[inputs.shape[0] - 1, :, :cols] = refs[2][0]
        inputs[inputs.shape[0] - 1, :, cols:] = refs[3][0]
    else:
        inputs[...] = jnp.zeros(inputs.shape, BF16)
    count = factors.shape[0] // 2
    for above in range(count):
        kept[begin + above] = factors[2 + 2 * above]
    kept[begin + count] = factors[0]
    onward[...] = next_factors[...]


def hold(level, factors, next_factors, before):
    size = factors.shape[1]
    vmem = pl.BlockSpec(memory_space=pltpu.VMEM)
    blocks = factors.shape[0] // 2 + 1 + (before[0].shape[0] if before else 0)
    cols = 2 * before[2].shape[2] if before else size
    *held, onward = pl.pallas_call(
        functools.partial(hold_kernel, len(before) // 4),
        in_specs=[vmem] * (2 + len(before)),
        out_specs=[vmem] * 3,
        out_shape=[
            jax.ShapeDtypeStruct((blocks, size, size), BF16),
            jax.ShapeDtypeStruct((max(level - 1, 1), size, cols), BF16),
            jax.ShapeDtypeStruct(next_factors.shape, BF16),
        ],
        compiler_params=pltpu.CompilerParams(vmem_limit_bytes=TREE_VMEM),
        cost_estimate=cost(2**20, 2**20),
        name="hold",
    )(factors, next_factors, *before)
    return held, onward


def descend_kernel(own, far, theirs, across, top, kept, inputs, paths):
    levels = paths.shape[0]
    entered = [own[1].astype(F32) + theirs[0].astype(F32), far[1].astype(F32) + across[0].astype(F32)]
    entered = (-jnp.concatenate(entered, axis=1)).astype(BF16)
    paths[levels - 1] = dot(top[0], entered).astype(BF16)
    end = kept.shape[0]
    for level in range(levels - 2, -1, -1):
        count = levels - 1 - level
        end -= count + 1
        if level == levels - 2:
            entered = jnp.concatenate([own[0], far[0]], axis=1)
        else:
            entered = inputs[level]
        rest = dot(kept[end + count], entered)
        for above in reversed(range(count)):
            rest = rest - dot(kept[end + above], paths[level + 1 + above])
        paths[level] = rest.astype(BF16)


def descend(levels, own, far, theirs, across, top, kept, inputs):
    _, size, cols = own.shape
    vmem = pl.BlockSpec(memory_space=pltpu.VMEM)
    return pl.pallas_call(
        descend_kernel,
        in_specs=[vmem] * 7,
        out_specs=vmem,
        out_shape=jax.ShapeDtypeStruct((levels, size, 2 * cols), BF16),
        compiler_params=pltpu.CompilerParams(vmem_limit_bytes=TREE_VMEM),
        cost_estimate=cost(2**20, 2**20),
        name="descend",
    )(own, far, theirs, across, top, kept, inputs)


def on_device(
    leaf_rhs,
    leaf_lower_inv,
    leaf_lower_panels,
    leaf_upper_inv,
    leaf_upper_panels,
    ancestors,
    sep_rhs,
    sep_lower_inv,
    sep_lower_panels,
    sep_upper_inv,
    sep_upper_panels,
):
    levels = lax.axis_size("leaf").bit_length() - 1
    device = lax.axis_index("leaf")
    place = lax.axis_index("col")
    low, high = place % 2, place // 2
    count = leaf_lower_inv.shape[0]
    rows, size, cols = leaf_rhs.shape

    first = high * 2 * count + low * count
    second = high * 2 * count + (1 - low) * count
    owned = [device % 2**level == 2 ** (level - 1) for level in range(1, levels + 1)]
    own_level = sum(jnp.where(is_owner, level, 0) for level, is_owner in enumerate(owned, 1))

    away = (1 - high) * 2 * count
    scalars = jnp.stack([first, second, own_level, away + low * count, away + (1 - low) * count]).astype(jnp.int32)
    half = count // 2
    sent = [lax.dynamic_slice_in_dim(leaf_rhs, away + low * count, count, 0)]
    sent.append(lax.dynamic_slice_in_dim(after(leaf_rhs, sent[0]), away + (1 - low) * count, count, 0))
    far_rhs = [swap(part, "col", 2) for part in sent]

    near_ancestors = swap(ancestors, "col", 1)
    near_lower_inv = swap(after(leaf_lower_inv, sent[0]), "col", 1)
    near_lower_panels = swap(after(leaf_lower_panels, sent[0]), "col", 1)
    local = (ancestors, leaf_lower_inv, leaf_lower_panels)
    near = (near_ancestors, near_lower_inv, near_lower_panels)

    blocks, pieces = combine(after(sep_lower_inv, *sent), sep_lower_panels, sep_upper_inv, sep_upper_panels)

    start = after(sep_rhs, *near)
    value_2_own, total = forward(levels, scalars, 1, *near, leaf_rhs, None, start, True, [F32])
    value_1, own_total, total = forward(levels, scalars, 0, *local, leaf_rhs, far_rhs[0], total, False, [BF16, F32])
    arrived = [swap(piece, "leaf", 1) for piece in pieces]
    count_above = blocks.shape[0] - 2
    onward = sort(device % 2, 0, blocks, after(arrived, total), (count_above, 1)) if levels > 1 else []
    total = after(total, *onward)
    value_2_far, far_total = forward(levels, scalars, 1, *near, None, far_rhs[1], total, False, [BF16])

    if levels == 3:
        from_top = [from_owners(onward[1], levels, hop) for hop in (4, 6)]
        far_total = after(far_total, *from_top)
    mine = (own_total.astype(F32) + swap(far_total, "col", 2).astype(F32)).astype(BF16)
    if levels == 3:
        from_top = pick(device // 2 % 2, from_top)
        mine = after(mine, from_top)
    (factors,) = sort(device % 2, 1, blocks, after(arrived, mine), (blocks.shape[0],))
    held = []
    for level in range(1, levels):
        theirs = swap(mine, "leaf", 2 ** (level - 1))
        here = onward[0]
        if levels != 3 or level == 1:
            arrived = swap(here, "leaf", 2**level)
            (following,) = sort(device // 2**level % 2, 1, here, [arrived], (here.shape[0],))
        if level < levels - 1 and levels != 3:
            onward = sort(device // 2**level % 2, 0, here, [arrived], (here.shape[0] - 2, 1))
        if levels == 3 and level == 1:
            (candidate,) = sort(device // 2 % 2, 0, here, [arrived], (1,))
            theirs = after(theirs, following, candidate)
            top = pick(device // 4 % 2, [from_top, candidate])
        elif levels == 3:
            following = top
            theirs = after(theirs, top)
        else:
            theirs = after(theirs, following)
        passed, entered = climb(mine, theirs, factors)
        if level == 1:
            near_upper_inv = swap(after(leaf_upper_inv, passed), "col", 1)
            near_upper_panels = swap(after(leaf_upper_panels, passed), "col", 1)
        held, following = hold(level, after(factors, passed), following, [*held, own, far] if level > 1 else [])
        mine, factors, own, far = passed, following, entered, swap(entered, "col", 2)
    theirs = swap(mine, "leaf", 2 ** (levels - 1))
    hop = 2 ** (levels - 1) * lax.axis_size("col") + 2
    pairs = [(source, source ^ hop) for source in range(lax.axis_size("leaf") * lax.axis_size("col"))]
    across = lax.ppermute(mine, ("leaf", "col"), pairs)
    paths = descend(levels, own, far, theirs, across, factors, *held)

    own_solution = jnp.zeros((size, cols), BF16)
    for level in range(levels):
        own_solution = jnp.where(owned[level], paths[level, :, :cols], own_solution)

    local = (ancestors, leaf_upper_inv, leaf_upper_panels)
    near = (near_ancestors, near_upper_inv, near_upper_panels)
    leaf_solution = solve_own(scalars, 0, *local, value_1, paths, rows)
    quarter = half // 2
    returning = [
        (3, 0, solve_far(*local, value_1, paths, 0, count - quarter)),
        (4, 0, solve_far(*near, value_2_far, paths, 0, half)),
        (4, half, solve_far(*near, value_2_far, paths, half, half)),
        (3, count - quarter, solve_far(*local, value_1, paths, count - quarter, quarter)),
    ]
    leaf_solution = solve_own(scalars, 1, *near, value_2_own, paths, rows, leaf_solution)
    for which, offset, part in returning:
        leaf_solution = place_rows(scalars, which, offset, swap(part, "col", 2), leaf_solution)
    return (leaf_solution, own_solution[None])


def solution(mesh):
    placed = (
        P("leaf", None, "col"),
        P(("leaf", "col"), None, None),
        P(("leaf", "col"), None, None, None),
        P(("leaf", "col"), None, None),
        P(("leaf", "col"), None, None, None),
        P(("leaf", "col"), None),
        P("leaf", None, "col"),
        P("leaf", None, None),
        P("leaf", None, None, None),
        P("leaf", None, None),
        P("leaf", None, None, None),
    )
    return jax.shard_map(
        on_device,
        mesh=mesh,
        in_specs=placed,
        out_specs=(P("leaf", None, "col"), P("leaf", None, "col")),
        check_vma=False,
    )
```

```python
import functools

import jax
import jax.numpy as jnp
from jax import lax
from jax.experimental import pallas as pl
from jax.experimental.pallas import tpu as pltpu
from jax.sharding import PartitionSpec as P

F32 = jnp.float32
BF16 = jnp.bfloat16
FORWARD_VMEM = 60 * 2**20
LEAF_VMEM = 10 * 2**20
TREE_VMEM = 6 * 2**20
BATCH = 4
PART = 3


def swap(value, axis, mask):
    pairs = [(source, source ^ mask) for source in range(lax.axis_size(axis))]
    return lax.ppermute(value, axis, pairs)


def dot(left, right):
    return jnp.dot(left, right, preferred_element_type=F32)


def cost(flops, moved):
    return pl.CostEstimate(flops=flops, bytes_accessed=moved, transcendentals=0)


def forward_kernel(own, far, first, scalars, ancestors, *refs):
    sides = own + far
    columns_in, (inv, panels, start) = refs[:sides], refs[sides : sides + 3]
    value, *totals = refs[sides + 3 : -3]
    solved, held, sems = refs[-3:]
    step, steps = pl.program_id(0), pl.num_programs(0)
    batch, slots = panels.shape[:2]
    levels = held.shape[0]
    cols = start.shape[2]

    def leaving(leaf):
        return pltpu.make_async_copy(solved.at[leaf], value.at[leaf], sems.at[leaf])

    @pl.when(step == 0)
    def _():
        if first:
            for level in range(levels):
                held[level] = start[0].astype(F32) * -(scalars[2] == level + 1).astype(F32)
        else:
            held[:, :, :cols] = start[...]
            if sides == 2:
                held[:, :, cols:] = jnp.zeros((levels, held.shape[1], cols), F32)

    values = []
    for leaf in range(batch):
        columns = [array[leaf] for array in columns_in]
        columns = jnp.concatenate(columns, axis=1) if sides == 2 else columns[0]
        values.append(dot(inv[leaf], columns).astype(BF16))
        solved[step * batch + leaf] = values[leaf]
        leaving(step * batch + leaf).start()
    sums = [None] * levels
    for leaf in range(batch):
        for slot in range(slots):
            product = dot(panels[leaf, slot], values[leaf])
            named = ancestors[step * batch + leaf, slot]
            for level in range(levels):
                term = product * (named == level + 1).astype(F32)
                sums[level] = term if sums[level] is None else sums[level] + term
    for level in range(levels):
        held[level] += sums[level]

    @pl.when(step == steps - 1)
    def _():
        for side, total in enumerate(totals):
            total[...] = held[:, :, side * cols : (side + 1) * cols].astype(total.dtype)
        for leaf in range(solved.shape[0]):
            leaving(leaf).wait()


def forward(levels, scalars, which, ancestors, inv, panels, rhs, far, start, first, types):
    count, size, _ = inv.shape
    cols = start.shape[2]
    slots = panels.shape[1]
    batch = min(BATCH, count)
    whole = lambda i, *_: (0, 0, 0)
    sides = [array for array in (rhs, far) if array is not None]
    specs = []
    if rhs is not None:
        specs.append(pl.BlockSpec((batch, size, cols), lambda i, scalars, _: (scalars[which] // batch + i, 0, 0)))
    if far is not None:
        specs.append(pl.BlockSpec((batch, size, cols), lambda i, *_: (i, 0, 0)))
    sums = [jax.ShapeDtypeStruct((levels, size, cols), kind) for kind in types]
    return pl.pallas_call(
        functools.partial(forward_kernel, rhs is not None, far is not None, first),
        grid_spec=pltpu.PrefetchScalarGridSpec(
            num_scalar_prefetch=2,
            grid=(count // batch,),
            in_specs=specs
            + [
                pl.BlockSpec((batch, size, size), lambda i, *_: (i, 0, 0)),
                pl.BlockSpec((batch, slots, size, size), lambda i, *_: (i, 0, 0, 0)),
                pl.BlockSpec(start.shape, whole),
            ],
            out_specs=[pl.BlockSpec(memory_space=pl.ANY)] + [pl.BlockSpec(part.shape, whole) for part in sums],
            scratch_shapes=[
                pltpu.VMEM((count, size, len(sides) * cols), BF16),
                pltpu.VMEM((levels, size, len(sides) * cols), F32),
                pltpu.SemaphoreType.DMA((count,)),
            ],
        ),
        out_shape=[jax.ShapeDtypeStruct((count, size, len(sides) * cols), BF16)] + sums,
        compiler_params=pltpu.CompilerParams(vmem_limit_bytes=FORWARD_VMEM),
        cost_estimate=cost(0, 0),
        name="leaf_forward",
    )(scalars, ancestors, *sides, inv, panels, start)


def solve_leaves(base, step, batch, ancestors, value, inv, panels, paths):
    leaves = [step * batch + index for index in range(batch)]
    rests = []
    for leaf in leaves:
        update = None
        for slot in range(panels.shape[1]):
            level = ancestors[base + leaf, slot]
            picked = paths[jnp.maximum(level - 1, 0)]
            picked = jnp.where(level > 0, picked, jnp.zeros_like(picked))
            term = dot(panels[leaf, slot], picked)
            update = term if update is None else update + term
        rests.append((value[leaf].astype(F32) - update).astype(BF16))
    return [dot(inv[leaf], rest).astype(BF16) for leaf, rest in zip(leaves, rests)]


def send_kernel(base, ancestors, value, inv, panels, paths, result):
    step = pl.program_id(0)
    batch = result.shape[0]
    solutions = solve_leaves(base + step * batch, 0, batch, ancestors, value, inv, panels, paths)
    for index, solution_block in enumerate(solutions):
        result[index] = solution_block


def solve_far(ancestors, inv, panels, value, paths, base, count):
    levels, size, cols = paths.shape[0], paths.shape[1], paths.shape[2] // 2
    batch = max(leaves for leaves in range(1, BATCH + 1) if count % leaves == 0 and base % leaves == 0)
    ahead = base // batch

    def part(array):
        block = (batch,) + array.shape[1:]
        return pl.BlockSpec(block, lambda i: (ahead + i,) + (0,) * (array.ndim - 1))

    return pl.pallas_call(
        functools.partial(send_kernel, base),
        grid=(count // batch,),
        in_specs=[
            pl.BlockSpec(memory_space=pltpu.SMEM),
            pl.BlockSpec((batch, size, cols), lambda i: (ahead + i, 0, value.shape[2] // cols - 1)),
            part(inv),
            part(panels),
            pl.BlockSpec((levels, size, cols), lambda i: (0, 0, 1)),
        ],
        out_specs=pl.BlockSpec((batch, size, cols), lambda i: (i, 0, 0)),
        out_shape=jax.ShapeDtypeStruct((count, size, cols), BF16),
        compiler_params=pltpu.CompilerParams(vmem_limit_bytes=LEAF_VMEM),
        cost_estimate=cost(0, 0),
        name="solve_far",
    )(ancestors, value, inv, panels, paths)


def keep_kernel(which, scalars, ancestors, value, inv, panels, paths, *refs):
    result, solved, sems = refs[-3:]
    step, steps = pl.program_id(0), pl.num_programs(0)
    batch = value.shape[0]

    def leaving(leaf):
        return pltpu.make_async_copy(solved.at[leaf], result.at[scalars[which] + leaf], sems.at[leaf])

    for index, solution_block in enumerate(solve_leaves(step * batch, 0, batch, ancestors, value, inv, panels, paths)):
        solved[step * batch + index] = solution_block
        leaving(step * batch + index).start()

    @pl.when(step == steps - 1)
    def _():
        for leaf in range(solved.shape[0]):
            leaving(leaf).wait()


def solve_own(scalars, which, ancestors, inv, panels, value, paths, rows, into=None):
    levels, size, cols = paths.shape[0], paths.shape[1], paths.shape[2] // 2
    count, slots = panels.shape[:2]
    batch = min(BATCH, count)
    extra = [] if into is None else [into]
    hbm, smem = pl.BlockSpec(memory_space=pl.ANY), pl.BlockSpec(memory_space=pltpu.SMEM)
    return pl.pallas_call(
        functools.partial(keep_kernel, which),
        grid=(count // batch,),
        in_specs=[
            smem,
            smem,
            pl.BlockSpec((batch, size, cols), lambda i: (i, 0, 0)),
            pl.BlockSpec((batch, size, size), lambda i: (i, 0, 0)),
            pl.BlockSpec((batch, slots, size, size), lambda i: (i, 0, 0, 0)),
            pl.BlockSpec((levels, size, cols), lambda i: (0, 0, 0)),
        ]
        + [hbm] * len(extra),
        out_specs=hbm,
        out_shape=jax.ShapeDtypeStruct((rows, size, cols), BF16),
        scratch_shapes=[pltpu.VMEM((count, size, cols), BF16), pltpu.SemaphoreType.DMA((count,))],
        input_output_aliases={} if into is None else {6: 0},
        compiler_params=pltpu.CompilerParams(vmem_limit_bytes=LEAF_VMEM),
        cost_estimate=cost(0, 0),
        name="solve_own",
    )(scalars, ancestors, value, inv, panels, paths, *extra)


def place_kernel(scalars, part, whole, result):
    result[...] = part[...]


def place_rows(scalars, which, offset, part, whole):
    count, size, cols = part.shape
    batch = max(leaves for leaves in (8, 4, 2, 1) if count % leaves == 0 and offset % leaves == 0)
    return pl.pallas_call(
        place_kernel,
        grid_spec=pltpu.PrefetchScalarGridSpec(
            num_scalar_prefetch=1,
            grid=(count // batch,),
            in_specs=[
                pl.BlockSpec(memory_space=pltpu.VMEM)
                if count == batch
                else pl.BlockSpec((batch, size, cols), lambda i, _: (i, 0, 0)),
                pl.BlockSpec(memory_space=pl.ANY),
            ],
            out_specs=pl.BlockSpec(
                (batch, size, cols), lambda i, scalars: ((scalars[which] + offset) // batch + i, 0, 0)
            ),
        ),
        out_shape=jax.ShapeDtypeStruct(whole.shape, whole.dtype),
        input_output_aliases={2: 0},
        compiler_params=pltpu.CompilerParams(vmem_limit_bytes=LEAF_VMEM),
        cost_estimate=cost(0, 0),
        name="place_rows",
    )(scalars, part, whole)


def combine_kernel(lower_inv, lower_panels, upper_inv, upper_panels, blocks, *parts):
    made = [dot(upper_inv[0], lower_inv[0]).astype(BF16)]
    for slot in range(blocks.shape[0] // 2):
        made.append(dot(lower_panels[0, slot], lower_inv[0]).astype(BF16))
        made.append(dot(upper_inv[0], upper_panels[0, slot]).astype(BF16))
    for index, block in enumerate(made):
        blocks[index] = block
    for part in parts:
        for index in range(part.shape[0]):
            part[index] = made.pop(0)


def combine(lower_inv, lower_panels, upper_inv, upper_panels):
    size = lower_inv.shape[1]
    total = 1 + 2 * lower_panels.shape[1]
    counts = [total] + [min(PART, total - begin) for begin in range(0, total, PART)]
    blocks, *parts = pl.pallas_call(
        combine_kernel,
        out_shape=[jax.ShapeDtypeStruct((blocks, size, size), BF16) for blocks in counts],
        compiler_params=pltpu.CompilerParams(vmem_limit_bytes=TREE_VMEM),
        cost_estimate=cost(2**20, 2**20),
        name="combine",
    )(lower_inv, lower_panels, upper_inv, upper_panels)
    return blocks, parts


def sort_kernel(parts, wanted, flags, mine, *refs):
    theirs, chosen = refs[:parts], refs[parts:]

    @pl.when(flags[0] == wanted)
    def _():
        for out in chosen:
            out[...] = mine[: out.shape[0]]

    @pl.when(flags[0] != wanted)
    def _():
        for out in chosen:
            begin = 0
            for part in theirs:
                for index in range(min(part.shape[0], out.shape[0] - begin)):
                    out[begin + index] = part[index]
                begin += part.shape[0]


def sort(bit, wanted, mine, theirs, counts):
    memory = pl.BlockSpec(memory_space=pltpu.VMEM)
    return pl.pallas_call(
        functools.partial(sort_kernel, len(theirs), wanted),
        in_specs=[pl.BlockSpec(memory_space=pltpu.SMEM), memory] + [memory] * len(theirs),
        out_specs=[memory] * len(counts),
        out_shape=[jax.ShapeDtypeStruct((count,) + mine.shape[1:], BF16) for count in counts],
        compiler_params=pltpu.CompilerParams(vmem_limit_bytes=TREE_VMEM),
        cost_estimate=cost(2**20, 2**20),
        name="sort",
    )(jnp.reshape(bit, (1,)).astype(jnp.int32), mine, *theirs)


def pick_kernel(flags, *refs):
    sources, chosen, sem = refs[:-2], refs[-2], refs[-1]
    for index, source in enumerate(sources):

        @pl.when(flags[0] == index)
        def _(source=source):
            copy = pltpu.make_async_copy(source.at[:1], chosen, sem)
            copy.start()
            copy.wait()


def pick(index, sources):
    return pl.pallas_call(
        pick_kernel,
        in_specs=[pl.BlockSpec(memory_space=pltpu.SMEM)] + [pl.BlockSpec(memory_space=pl.ANY)] * len(sources),
        out_specs=pl.BlockSpec(memory_space=pltpu.VMEM),
        out_shape=jax.ShapeDtypeStruct((1,) + sources[0].shape[1:], BF16),
        scratch_shapes=[pltpu.SemaphoreType.DMA],
        compiler_params=pltpu.CompilerParams(vmem_limit_bytes=FORWARD_VMEM),
        cost_estimate=cost(2**20, 2**20),
        name="pick",
    )(jnp.reshape(index, (1,)).astype(jnp.int32), *sources)


def from_owners(value, level, hop):
    owner = 2 ** (level - 1)
    pairs = [
        (group + owner + index, group + (owner + index ^ hop))
        for group in range(0, lax.axis_size("leaf"), 2**level)
        for index in range(2)
    ]
    return lax.ppermute(value, "leaf", pairs)


def after(value, *earlier):
    return lax.optimization_barrier((value, *earlier))[0]


def climb_kernel(mine, theirs, factors, passed, entered):
    here = (-(mine[0].astype(F32) + theirs[0].astype(F32))).astype(BF16)
    for above in range(passed.shape[0]):
        carried = mine[above + 1].astype(F32) + theirs[above + 1].astype(F32)
        passed[above] = (carried + dot(factors[1 + 2 * above], here)).astype(BF16)
    entered[0] = here


def climb(mine, theirs, factors):
    levels, size, cols = mine.shape
    vmem = pl.BlockSpec(memory_space=pltpu.VMEM)
    return pl.pallas_call(
        climb_kernel,
        in_specs=[vmem] * 3,
        out_specs=[vmem] * 2,
        out_shape=[
            jax.ShapeDtypeStruct((levels - 1, size, cols), BF16),
            jax.ShapeDtypeStruct((1, size, cols), BF16),
        ],
        compiler_params=pltpu.CompilerParams(vmem_limit_bytes=TREE_VMEM),
        cost_estimate=cost(2**20, 2**20),
        name="climb",
    )(mine, theirs, factors)


def hold_kernel(below, factors, next_factors, *refs):
    refs, (kept, inputs, onward) = refs[:-3], refs[-3:]
    begin = 0
    if below == 1:
        begin = refs[0].shape[0]
        kept[:begin] = refs[0][...]
        cols = refs[2].shape[2]
        if inputs.shape[0] > 1:
            inputs[:-1] = refs[1][...]
        inputs[inputs.shape[0] - 1, :, :cols] = refs[2][0]
        inputs[inputs.shape[0] - 1, :, cols:] = refs[3][0]
    else:
        inputs[...] = jnp.zeros(inputs.shape, BF16)
    count = factors.shape[0] // 2
    for above in range(count):
        kept[begin + above] = factors[2 + 2 * above]
    kept[begin + count] = factors[0]
    onward[...] = next_factors[...]


def hold(level, factors, next_factors, before):
    size = factors.shape[1]
    vmem = pl.BlockSpec(memory_space=pltpu.VMEM)
    blocks = factors.shape[0] // 2 + 1 + (before[0].shape[0] if before else 0)
    cols = 2 * before[2].shape[2] if before else size
    *held, onward = pl.pallas_call(
        functools.partial(hold_kernel, len(before) // 4),
        in_specs=[vmem] * (2 + len(before)),
        out_specs=[vmem] * 3,
        out_shape=[
            jax.ShapeDtypeStruct((blocks, size, size), BF16),
            jax.ShapeDtypeStruct((max(level - 1, 1), size, cols), BF16),
            jax.ShapeDtypeStruct(next_factors.shape, BF16),
        ],
        compiler_params=pltpu.CompilerParams(vmem_limit_bytes=TREE_VMEM),
        cost_estimate=cost(2**20, 2**20),
        name="hold",
    )(factors, next_factors, *before)
    return held, onward


def enter_kernel(mine, theirs, entered):
    entered[0] = (-(mine[0].astype(F32) + theirs[0].astype(F32))).astype(BF16)


def enter(mine, theirs):
    vmem = pl.BlockSpec(memory_space=pltpu.VMEM)
    return pl.pallas_call(
        enter_kernel,
        in_specs=[vmem] * 2,
        out_specs=vmem,
        out_shape=jax.ShapeDtypeStruct(mine.shape, BF16),
        compiler_params=pltpu.CompilerParams(vmem_limit_bytes=TREE_VMEM),
        cost_estimate=cost(2**20, 2**20),
        name="enter",
    )(mine, theirs)


def descend_kernel(own, far, own_top, far_top, top, kept, inputs, paths):
    levels = paths.shape[0]
    paths[levels - 1] = dot(top[0], jnp.concatenate([own_top[0], far_top[0]], axis=1)).astype(BF16)
    end = kept.shape[0]
    for level in range(levels - 2, -1, -1):
        count = levels - 1 - level
        end -= count + 1
        if level == levels - 2:
            entered = jnp.concatenate([own[0], far[0]], axis=1)
        else:
            entered = inputs[level]
        rest = dot(kept[end + count], entered)
        for above in reversed(range(count)):
            rest = rest - dot(kept[end + above], paths[level + 1 + above])
        paths[level] = rest.astype(BF16)


def descend(levels, own, far, own_top, far_top, top, kept, inputs):
    _, size, cols = own.shape
    vmem = pl.BlockSpec(memory_space=pltpu.VMEM)
    return pl.pallas_call(
        descend_kernel,
        in_specs=[vmem] * 7,
        out_specs=vmem,
        out_shape=jax.ShapeDtypeStruct((levels, size, 2 * cols), BF16),
        compiler_params=pltpu.CompilerParams(vmem_limit_bytes=TREE_VMEM),
        cost_estimate=cost(2**20, 2**20),
        name="descend",
    )(own, far, own_top, far_top, top, kept, inputs)


def on_device(
    leaf_rhs,
    leaf_lower_inv,
    leaf_lower_panels,
    leaf_upper_inv,
    leaf_upper_panels,
    ancestors,
    sep_rhs,
    sep_lower_inv,
    sep_lower_panels,
    sep_upper_inv,
    sep_upper_panels,
):
    levels = lax.axis_size("leaf").bit_length() - 1
    device = lax.axis_index("leaf")
    place = lax.axis_index("col")
    low, high = place % 2, place // 2
    count = leaf_lower_inv.shape[0]
    rows, size, cols = leaf_rhs.shape

    first = high * 2 * count + low * count
    second = high * 2 * count + (1 - low) * count
    owned = [device % 2**level == 2 ** (level - 1) for level in range(1, levels + 1)]
    own_level = sum(jnp.where(is_owner, level, 0) for level, is_owner in enumerate(owned, 1))

    away = (1 - high) * 2 * count
    scalars = jnp.stack([first, second, own_level, away + low * count, away + (1 - low) * count]).astype(jnp.int32)
    half = count // 2
    sent = [lax.dynamic_slice_in_dim(leaf_rhs, away + low * count, count, 0)]
    sent.append(lax.dynamic_slice_in_dim(after(leaf_rhs, sent[0]), away + (1 - low) * count, count, 0))
    far_rhs = [swap(part, "col", 2) for part in sent]

    near_ancestors = swap(ancestors, "col", 1)
    near_lower_inv = swap(after(leaf_lower_inv, sent[0]), "col", 1)
    near_lower_panels = swap(after(leaf_lower_panels, sent[0]), "col", 1)
    local = (ancestors, leaf_lower_inv, leaf_lower_panels)
    near = (near_ancestors, near_lower_inv, near_lower_panels)

    blocks, pieces = combine(after(sep_lower_inv, *sent), sep_lower_panels, sep_upper_inv, sep_upper_panels)

    start = after(sep_rhs, *near)
    value_2_own, total = forward(levels, scalars, 1, *near, leaf_rhs, None, start, True, [F32])
    value_1, own_total, total = forward(levels, scalars, 0, *local, leaf_rhs, far_rhs[0], total, False, [BF16, F32])
    arrived = [swap(piece, "leaf", 1) for piece in pieces]
    count_above = blocks.shape[0] - 2
    onward = sort(device % 2, 0, blocks, after(arrived, total), (count_above, 1)) if levels > 1 else []
    total = after(total, *onward)
    value_2_far, far_total = forward(levels, scalars, 1, *near, None, far_rhs[1], total, False, [BF16])

    if levels == 3:
        from_top = [from_owners(onward[1], levels, hop) for hop in (4, 6)]
        far_total = after(far_total, *from_top)
    mine = (own_total.astype(F32) + swap(far_total, "col", 2).astype(F32)).astype(BF16)
    if levels == 3:
        from_top = pick(device // 2 % 2, from_top)
        mine = after(mine, from_top)
    (factors,) = sort(device % 2, 1, blocks, after(arrived, mine), (blocks.shape[0],))
    held = []
    for level in range(1, levels):
        theirs = swap(mine, "leaf", 2 ** (level - 1))
        here = onward[0]
        if levels != 3 or level == 1:
            arrived = swap(here, "leaf", 2**level)
            (following,) = sort(device // 2**level % 2, 1, here, [arrived], (here.shape[0],))
        if level < levels - 1 and levels != 3:
            onward = sort(device // 2**level % 2, 0, here, [arrived], (here.shape[0] - 2, 1))
        if levels == 3 and level == 1:
            (candidate,) = sort(device // 2 % 2, 0, here, [arrived], (1,))
            theirs = after(theirs, following, candidate)
            top = pick(device // 4 % 2, [from_top, candidate])
        elif levels == 3:
            following = top
            theirs = after(theirs, top)
        else:
            theirs = after(theirs, following)
        passed, entered = climb(mine, theirs, factors)
        if level == levels - 1:
            near_upper_inv = swap(after(leaf_upper_inv, passed), "col", 1)
            near_upper_panels = swap(after(leaf_upper_panels, passed), "col", 1)
        held, following = hold(level, after(factors, passed), following, [*held, own, far] if level > 1 else [])
        mine, factors, own, far = passed, following, entered, swap(entered, "col", 2)
    theirs = swap(mine, "leaf", 2 ** (levels - 1))
    own_top = enter(mine, theirs)
    paths = descend(levels, own, far, own_top, swap(own_top, "col", 2), factors, *held)

    own_solution = jnp.zeros((size, cols), BF16)
    for level in range(levels):
        own_solution = jnp.where(owned[level], paths[level, :, :cols], own_solution)

    local = (ancestors, leaf_upper_inv, leaf_upper_panels)
    near = (near_ancestors, near_upper_inv, near_upper_panels)
    leaf_solution = solve_own(scalars, 0, *local, value_1, paths, rows)
    quarter = half // 2
    returning = [
        (3, 0, solve_far(*local, value_1, paths, 0, count - quarter)),
        (4, 0, solve_far(*near, value_2_far, paths, 0, half)),
        (4, half, solve_far(*near, value_2_far, paths, half, half)),
        (3, count - quarter, solve_far(*local, value_1, paths, count - quarter, quarter)),
    ]
    leaf_solution = solve_own(scalars, 1, *near, value_2_own, paths, rows, leaf_solution)
    for which, offset, part in returning:
        leaf_solution = place_rows(scalars, which, offset, swap(part, "col", 2), leaf_solution)
    return (leaf_solution, own_solution[None])


def solution(mesh):
    placed = (
        P("leaf", None, "col"),
        P(("leaf", "col"), None, None),
        P(("leaf", "col"), None, None, None),
        P(("leaf", "col"), None, None),
        P(("leaf", "col"), None, None, None),
        P(("leaf", "col"), None),
        P("leaf", None, "col"),
        P("leaf", None, None),
        P("leaf", None, None, None),
        P("leaf", None, None),
        P("leaf", None, None, None),
    )
    return jax.shard_map(
        on_device,
        mesh=mesh,
        in_specs=placed,
        out_specs=(P("leaf", None, "col"), P("leaf", None, "col")),
        check_vma=False,
    )
```

```python
import functools

import jax
import jax.numpy as jnp
from jax import lax
from jax.experimental import pallas as pl
from jax.experimental.pallas import tpu as pltpu
from jax.sharding import PartitionSpec as P

F32 = jnp.float32
BF16 = jnp.bfloat16
FORWARD_VMEM = 60 * 2**20
LEAF_VMEM = 10 * 2**20
TREE_VMEM = 6 * 2**20
BATCH = 4
SOLVE_BATCH = 6
PART = 3


def swap(value, axis, mask):
    pairs = [(source, source ^ mask) for source in range(lax.axis_size(axis))]
    return lax.ppermute(value, axis, pairs)


def dot(left, right):
    return jnp.dot(left, right, preferred_element_type=F32)


def cost(flops, moved):
    return pl.CostEstimate(flops=flops, bytes_accessed=moved, transcendentals=0)


def forward_kernel(own, far, first, scalars, ancestors, *refs):
    sides = own + far
    columns_in, (inv, panels, start) = refs[:sides], refs[sides : sides + 3]
    value, *totals = refs[sides + 3 : -3]
    solved, held, sems = refs[-3:]
    step, steps = pl.program_id(0), pl.num_programs(0)
    batch, slots = panels.shape[:2]
    levels = held.shape[0]
    cols = start.shape[2]

    def leaving(leaf):
        return pltpu.make_async_copy(solved.at[leaf], value.at[leaf], sems.at[leaf])

    @pl.when(step == 0)
    def _():
        if first:
            for level in range(levels):
                held[level] = start[0].astype(F32) * -(scalars[2] == level + 1).astype(F32)
        else:
            held[:, :, :cols] = start[...]
            if sides == 2:
                held[:, :, cols:] = jnp.zeros((levels, held.shape[1], cols), F32)

    values = []
    for leaf in range(batch):
        columns = [array[leaf] for array in columns_in]
        columns = jnp.concatenate(columns, axis=1) if sides == 2 else columns[0]
        values.append(dot(inv[leaf], columns).astype(BF16))
        solved[step * batch + leaf] = values[leaf]
        leaving(step * batch + leaf).start()
    sums = [None] * levels
    for leaf in range(batch):
        for slot in range(slots):
            product = dot(panels[leaf, slot], values[leaf])
            named = ancestors[step * batch + leaf, slot]
            for level in range(levels):
                term = product * (named == level + 1).astype(F32)
                sums[level] = term if sums[level] is None else sums[level] + term
    for level in range(levels):
        held[level] += sums[level]

    @pl.when(step == steps - 1)
    def _():
        for side, total in enumerate(totals):
            total[...] = held[:, :, side * cols : (side + 1) * cols].astype(total.dtype)
        for leaf in range(solved.shape[0]):
            leaving(leaf).wait()


def forward(levels, scalars, which, ancestors, inv, panels, rhs, far, start, first, types):
    count, size, _ = inv.shape
    cols = start.shape[2]
    slots = panels.shape[1]
    batch = min(BATCH, count)
    whole = lambda i, *_: (0, 0, 0)
    sides = [array for array in (rhs, far) if array is not None]
    specs = []
    if rhs is not None:
        specs.append(pl.BlockSpec((batch, size, cols), lambda i, scalars, _: (scalars[which] // batch + i, 0, 0)))
    if far is not None:
        specs.append(pl.BlockSpec((batch, size, cols), lambda i, *_: (i, 0, 0)))
    sums = [jax.ShapeDtypeStruct((levels, size, cols), kind) for kind in types]
    return pl.pallas_call(
        functools.partial(forward_kernel, rhs is not None, far is not None, first),
        grid_spec=pltpu.PrefetchScalarGridSpec(
            num_scalar_prefetch=2,
            grid=(count // batch,),
            in_specs=specs
            + [
                pl.BlockSpec((batch, size, size), lambda i, *_: (i, 0, 0)),
                pl.BlockSpec((batch, slots, size, size), lambda i, *_: (i, 0, 0, 0)),
                pl.BlockSpec(start.shape, whole),
            ],
            out_specs=[pl.BlockSpec(memory_space=pl.ANY)] + [pl.BlockSpec(part.shape, whole) for part in sums],
            scratch_shapes=[
                pltpu.VMEM((count, size, len(sides) * cols), BF16),
                pltpu.VMEM((levels, size, len(sides) * cols), F32),
                pltpu.SemaphoreType.DMA((count,)),
            ],
        ),
        out_shape=[jax.ShapeDtypeStruct((count, size, len(sides) * cols), BF16)] + sums,
        compiler_params=pltpu.CompilerParams(vmem_limit_bytes=FORWARD_VMEM),
        cost_estimate=cost(0, 0),
        name="leaf_forward",
    )(scalars, ancestors, *sides, inv, panels, start)


def solve_leaves(base, step, batch, ancestors, value, inv, panels, paths):
    leaves = [step * batch + index for index in range(batch)]
    rests = []
    for leaf in leaves:
        update = None
        for slot in range(panels.shape[1]):
            level = ancestors[base + leaf, slot]
            picked = paths[jnp.maximum(level - 1, 0)]
            picked = jnp.where(level > 0, picked, jnp.zeros_like(picked))
            term = dot(panels[leaf, slot], picked)
            update = term if update is None else update + term
        rests.append((value[leaf].astype(F32) - update).astype(BF16))
    return [dot(inv[leaf], rest).astype(BF16) for leaf, rest in zip(leaves, rests)]


def send_kernel(base, ancestors, value, inv, panels, paths, result):
    step = pl.program_id(0)
    batch = result.shape[0]
    solutions = solve_leaves(base + step * batch, 0, batch, ancestors, value, inv, panels, paths)
    for index, solution_block in enumerate(solutions):
        result[index] = solution_block


def solve_far(ancestors, inv, panels, value, paths, base, count):
    levels, size, cols = paths.shape[0], paths.shape[1], paths.shape[2] // 2
    batch = max(leaves for leaves in range(1, SOLVE_BATCH + 1) if count % leaves == 0 and base % leaves == 0)
    ahead = base // batch

    def part(array):
        block = (batch,) + array.shape[1:]
        return pl.BlockSpec(block, lambda i: (ahead + i,) + (0,) * (array.ndim - 1))

    return pl.pallas_call(
        functools.partial(send_kernel, base),
        grid=(count // batch,),
        in_specs=[
            pl.BlockSpec(memory_space=pltpu.SMEM),
            pl.BlockSpec((batch, size, cols), lambda i: (ahead + i, 0, value.shape[2] // cols - 1)),
            part(inv),
            part(panels),
            pl.BlockSpec((levels, size, cols), lambda i: (0, 0, 1)),
        ],
        out_specs=pl.BlockSpec((batch, size, cols), lambda i: (i, 0, 0)),
        out_shape=jax.ShapeDtypeStruct((count, size, cols), BF16),
        compiler_params=pltpu.CompilerParams(vmem_limit_bytes=LEAF_VMEM),
        cost_estimate=cost(0, 0),
        name="solve_far",
    )(ancestors, value, inv, panels, paths)


def keep_kernel(which, scalars, ancestors, value, inv, panels, paths, *refs):
    result, solved, sems = refs[-3:]
    step, steps = pl.program_id(0), pl.num_programs(0)
    batch = value.shape[0]

    def leaving(leaf):
        return pltpu.make_async_copy(solved.at[leaf], result.at[scalars[which] + leaf], sems.at[leaf])

    for index, solution_block in enumerate(solve_leaves(step * batch, 0, batch, ancestors, value, inv, panels, paths)):
        solved[step * batch + index] = solution_block
        leaving(step * batch + index).start()

    @pl.when(step == steps - 1)
    def _():
        for leaf in range(solved.shape[0]):
            leaving(leaf).wait()


def solve_own(scalars, which, ancestors, inv, panels, value, paths, rows, into=None):
    levels, size, cols = paths.shape[0], paths.shape[1], paths.shape[2] // 2
    count, slots = panels.shape[:2]
    batch = min(BATCH, count)
    extra = [] if into is None else [into]
    hbm, smem = pl.BlockSpec(memory_space=pl.ANY), pl.BlockSpec(memory_space=pltpu.SMEM)
    return pl.pallas_call(
        functools.partial(keep_kernel, which),
        grid=(count // batch,),
        in_specs=[
            smem,
            smem,
            pl.BlockSpec((batch, size, cols), lambda i: (i, 0, 0)),
            pl.BlockSpec((batch, size, size), lambda i: (i, 0, 0)),
            pl.BlockSpec((batch, slots, size, size), lambda i: (i, 0, 0, 0)),
            pl.BlockSpec((levels, size, cols), lambda i: (0, 0, 0)),
        ]
        + [hbm] * len(extra),
        out_specs=hbm,
        out_shape=jax.ShapeDtypeStruct((rows, size, cols), BF16),
        scratch_shapes=[pltpu.VMEM((count, size, cols), BF16), pltpu.SemaphoreType.DMA((count,))],
        input_output_aliases={} if into is None else {6: 0},
        compiler_params=pltpu.CompilerParams(vmem_limit_bytes=LEAF_VMEM),
        cost_estimate=cost(0, 0),
        name="solve_own",
    )(scalars, ancestors, value, inv, panels, paths, *extra)


def place_kernel(scalars, part, whole, result):
    result[...] = part[...]


def place_rows(scalars, which, offset, part, whole):
    count, size, cols = part.shape
    batch = max(leaves for leaves in (8, 4, 2, 1) if count % leaves == 0 and offset % leaves == 0)
    return pl.pallas_call(
        place_kernel,
        grid_spec=pltpu.PrefetchScalarGridSpec(
            num_scalar_prefetch=1,
            grid=(count // batch,),
            in_specs=[
                pl.BlockSpec(memory_space=pltpu.VMEM)
                if count == batch
                else pl.BlockSpec((batch, size, cols), lambda i, _: (i, 0, 0)),
                pl.BlockSpec(memory_space=pl.ANY),
            ],
            out_specs=pl.BlockSpec(
                (batch, size, cols), lambda i, scalars: ((scalars[which] + offset) // batch + i, 0, 0)
            ),
        ),
        out_shape=jax.ShapeDtypeStruct(whole.shape, whole.dtype),
        input_output_aliases={2: 0},
        compiler_params=pltpu.CompilerParams(vmem_limit_bytes=LEAF_VMEM),
        cost_estimate=cost(0, 0),
        name="place_rows",
    )(scalars, part, whole)


def combine_kernel(lower_inv, lower_panels, upper_inv, upper_panels, blocks, *parts):
    made = [dot(upper_inv[0], lower_inv[0]).astype(BF16)]
    for slot in range(blocks.shape[0] // 2):
        made.append(dot(lower_panels[0, slot], lower_inv[0]).astype(BF16))
        made.append(dot(upper_inv[0], upper_panels[0, slot]).astype(BF16))
    for index, block in enumerate(made):
        blocks[index] = block
    for part in parts:
        for index in range(part.shape[0]):
            part[index] = made.pop(0)


def combine(lower_inv, lower_panels, upper_inv, upper_panels):
    size = lower_inv.shape[1]
    total = 1 + 2 * lower_panels.shape[1]
    counts = [total] + [min(PART, total - begin) for begin in range(0, total, PART)]
    blocks, *parts = pl.pallas_call(
        combine_kernel,
        out_shape=[jax.ShapeDtypeStruct((blocks, size, size), BF16) for blocks in counts],
        compiler_params=pltpu.CompilerParams(vmem_limit_bytes=TREE_VMEM),
        cost_estimate=cost(2**20, 2**20),
        name="combine",
    )(lower_inv, lower_panels, upper_inv, upper_panels)
    return blocks, parts


def sort_kernel(parts, wanted, flags, mine, *refs):
    theirs, chosen = refs[:parts], refs[parts:]

    @pl.when(flags[0] == wanted)
    def _():
        for out in chosen:
            out[...] = mine[: out.shape[0]]

    @pl.when(flags[0] != wanted)
    def _():
        for out in chosen:
            begin = 0
            for part in theirs:
                for index in range(min(part.shape[0], out.shape[0] - begin)):
                    out[begin + index] = part[index]
                begin += part.shape[0]


def sort(bit, wanted, mine, theirs, counts):
    memory = pl.BlockSpec(memory_space=pltpu.VMEM)
    return pl.pallas_call(
        functools.partial(sort_kernel, len(theirs), wanted),
        in_specs=[pl.BlockSpec(memory_space=pltpu.SMEM), memory] + [memory] * len(theirs),
        out_specs=[memory] * len(counts),
        out_shape=[jax.ShapeDtypeStruct((count,) + mine.shape[1:], BF16) for count in counts],
        compiler_params=pltpu.CompilerParams(vmem_limit_bytes=TREE_VMEM),
        cost_estimate=cost(2**20, 2**20),
        name="sort",
    )(jnp.reshape(bit, (1,)).astype(jnp.int32), mine, *theirs)


def pick_kernel(flags, *refs):
    sources, chosen, sem = refs[:-2], refs[-2], refs[-1]
    for index, source in enumerate(sources):

        @pl.when(flags[0] == index)
        def _(source=source):
            copy = pltpu.make_async_copy(source.at[:1], chosen, sem)
            copy.start()
            copy.wait()


def pick(index, sources):
    return pl.pallas_call(
        pick_kernel,
        in_specs=[pl.BlockSpec(memory_space=pltpu.SMEM)] + [pl.BlockSpec(memory_space=pl.ANY)] * len(sources),
        out_specs=pl.BlockSpec(memory_space=pltpu.VMEM),
        out_shape=jax.ShapeDtypeStruct((1,) + sources[0].shape[1:], BF16),
        scratch_shapes=[pltpu.SemaphoreType.DMA],
        compiler_params=pltpu.CompilerParams(vmem_limit_bytes=FORWARD_VMEM),
        cost_estimate=cost(2**20, 2**20),
        name="pick",
    )(jnp.reshape(index, (1,)).astype(jnp.int32), *sources)


def from_owners(value, level, hop):
    owner = 2 ** (level - 1)
    pairs = [
        (group + owner + index, group + (owner + index ^ hop))
        for group in range(0, lax.axis_size("leaf"), 2**level)
        for index in range(2)
    ]
    return lax.ppermute(value, "leaf", pairs)


def after(value, *earlier):
    return lax.optimization_barrier((value, *earlier))[0]


def climb_kernel(mine, theirs, factors, passed, entered):
    here = (-(mine[0].astype(F32) + theirs[0].astype(F32))).astype(BF16)
    for above in range(passed.shape[0]):
        carried = mine[above + 1].astype(F32) + theirs[above + 1].astype(F32)
        passed[above] = (carried + dot(factors[1 + 2 * above], here)).astype(BF16)
    entered[0] = here


def climb(mine, theirs, factors):
    levels, size, cols = mine.shape
    vmem = pl.BlockSpec(memory_space=pltpu.VMEM)
    return pl.pallas_call(
        climb_kernel,
        in_specs=[vmem] * 3,
        out_specs=[vmem] * 2,
        out_shape=[
            jax.ShapeDtypeStruct((levels - 1, size, cols), BF16),
            jax.ShapeDtypeStruct((1, size, cols), BF16),
        ],
        compiler_params=pltpu.CompilerParams(vmem_limit_bytes=TREE_VMEM),
        cost_estimate=cost(2**20, 2**20),
        name="climb",
    )(mine, theirs, factors)


def hold_kernel(below, factors, next_factors, *refs):
    refs, (kept, inputs, onward) = refs[:-3], refs[-3:]
    begin = 0
    if below == 1:
        begin = refs[0].shape[0]
        kept[:begin] = refs[0][...]
        cols = refs[2].shape[2]
        if inputs.shape[0] > 1:
            inputs[:-1] = refs[1][...]
        inputs[inputs.shape[0] - 1, :, :cols] = refs[2][0]
        inputs[inputs.shape[0] - 1, :, cols:] = refs[3][0]
    else:
        inputs[...] = jnp.zeros(inputs.shape, BF16)
    count = factors.shape[0] // 2
    for above in range(count):
        kept[begin + above] = factors[2 + 2 * above]
    kept[begin + count] = factors[0]
    onward[...] = next_factors[...]


def hold(level, factors, next_factors, before):
    size = factors.shape[1]
    vmem = pl.BlockSpec(memory_space=pltpu.VMEM)
    blocks = factors.shape[0] // 2 + 1 + (before[0].shape[0] if before else 0)
    cols = 2 * before[2].shape[2] if before else size
    *held, onward = pl.pallas_call(
        functools.partial(hold_kernel, len(before) // 4),
        in_specs=[vmem] * (2 + len(before)),
        out_specs=[vmem] * 3,
        out_shape=[
            jax.ShapeDtypeStruct((blocks, size, size), BF16),
            jax.ShapeDtypeStruct((max(level - 1, 1), size, cols), BF16),
            jax.ShapeDtypeStruct(next_factors.shape, BF16),
        ],
        compiler_params=pltpu.CompilerParams(vmem_limit_bytes=TREE_VMEM),
        cost_estimate=cost(2**20, 2**20),
        name="hold",
    )(factors, next_factors, *before)
    return held, onward


def enter_kernel(mine, theirs, entered):
    entered[0] = (-(mine[0].astype(F32) + theirs[0].astype(F32))).astype(BF16)


def enter(mine, theirs):
    vmem = pl.BlockSpec(memory_space=pltpu.VMEM)
    return pl.pallas_call(
        enter_kernel,
        in_specs=[vmem] * 2,
        out_specs=vmem,
        out_shape=jax.ShapeDtypeStruct(mine.shape, BF16),
        compiler_params=pltpu.CompilerParams(vmem_limit_bytes=TREE_VMEM),
        cost_estimate=cost(2**20, 2**20),
        name="enter",
    )(mine, theirs)


def descend_kernel(own, far, own_top, far_top, top, kept, inputs, paths):
    levels = paths.shape[0]
    paths[levels - 1] = dot(top[0], jnp.concatenate([own_top[0], far_top[0]], axis=1)).astype(BF16)
    end = kept.shape[0]
    for level in range(levels - 2, -1, -1):
        count = levels - 1 - level
        end -= count + 1
        if level == levels - 2:
            entered = jnp.concatenate([own[0], far[0]], axis=1)
        else:
            entered = inputs[level]
        rest = dot(kept[end + count], entered)
        for above in reversed(range(count)):
            rest = rest - dot(kept[end + above], paths[level + 1 + above])
        paths[level] = rest.astype(BF16)


def descend(levels, own, far, own_top, far_top, top, kept, inputs):
    _, size, cols = own.shape
    vmem = pl.BlockSpec(memory_space=pltpu.VMEM)
    return pl.pallas_call(
        descend_kernel,
        in_specs=[vmem] * 7,
        out_specs=vmem,
        out_shape=jax.ShapeDtypeStruct((levels, size, 2 * cols), BF16),
        compiler_params=pltpu.CompilerParams(vmem_limit_bytes=TREE_VMEM),
        cost_estimate=cost(2**20, 2**20),
        name="descend",
    )(own, far, own_top, far_top, top, kept, inputs)


def on_device(
    leaf_rhs,
    leaf_lower_inv,
    leaf_lower_panels,
    leaf_upper_inv,
    leaf_upper_panels,
    ancestors,
    sep_rhs,
    sep_lower_inv,
    sep_lower_panels,
    sep_upper_inv,
    sep_upper_panels,
):
    levels = lax.axis_size("leaf").bit_length() - 1
    device = lax.axis_index("leaf")
    place = lax.axis_index("col")
    low, high = place % 2, place // 2
    count = leaf_lower_inv.shape[0]
    rows, size, cols = leaf_rhs.shape

    first = high * 2 * count + low * count
    second = high * 2 * count + (1 - low) * count
    owned = [device % 2**level == 2 ** (level - 1) for level in range(1, levels + 1)]
    own_level = sum(jnp.where(is_owner, level, 0) for level, is_owner in enumerate(owned, 1))

    away = (1 - high) * 2 * count
    scalars = jnp.stack([first, second, own_level, away + low * count, away + (1 - low) * count]).astype(jnp.int32)
    half = count // 2
    sent = [lax.dynamic_slice_in_dim(leaf_rhs, away + low * count, count, 0)]
    sent.append(lax.dynamic_slice_in_dim(after(leaf_rhs, sent[0]), away + (1 - low) * count, count, 0))
    far_rhs = [swap(part, "col", 2) for part in sent]

    near_ancestors = swap(ancestors, "col", 1)
    near_lower_inv = swap(after(leaf_lower_inv, sent[0]), "col", 1)
    near_lower_panels = swap(after(leaf_lower_panels, sent[0]), "col", 1)
    local = (ancestors, leaf_lower_inv, leaf_lower_panels)
    near = (near_ancestors, near_lower_inv, near_lower_panels)

    blocks, pieces = combine(after(sep_lower_inv, *sent), sep_lower_panels, sep_upper_inv, sep_upper_panels)

    start = after(sep_rhs, *near)
    value_2_own, total = forward(levels, scalars, 1, *near, leaf_rhs, None, start, True, [F32])
    value_1, own_total, total = forward(levels, scalars, 0, *local, leaf_rhs, far_rhs[0], total, False, [BF16, F32])
    arrived = [swap(piece, "leaf", 1) for piece in pieces]
    count_above = blocks.shape[0] - 2
    onward = sort(device % 2, 0, blocks, after(arrived, total), (count_above, 1)) if levels > 1 else []
    total = after(total, *onward)
    value_2_far, far_total = forward(levels, scalars, 1, *near, None, far_rhs[1], total, False, [BF16])

    if levels == 3:
        from_top = [from_owners(onward[1], levels, hop) for hop in (4, 6)]
        far_total = after(far_total, *from_top)
    mine = (own_total.astype(F32) + swap(far_total, "col", 2).astype(F32)).astype(BF16)
    if levels == 3:
        from_top = pick(device // 2 % 2, from_top)
        mine = after(mine, from_top)
    (factors,) = sort(device % 2, 1, blocks, after(arrived, mine), (blocks.shape[0],))
    held = []
    for level in range(1, levels):
        theirs = swap(mine, "leaf", 2 ** (level - 1))
        here = onward[0]
        if levels != 3 or level == 1:
            arrived = swap(here, "leaf", 2**level)
            (following,) = sort(device // 2**level % 2, 1, here, [arrived], (here.shape[0],))
        if level < levels - 1 and levels != 3:
            onward = sort(device // 2**level % 2, 0, here, [arrived], (here.shape[0] - 2, 1))
        if levels == 3 and level == 1:
            (candidate,) = sort(device // 2 % 2, 0, here, [arrived], (1,))
            theirs = after(theirs, following, candidate)
            top = pick(device // 4 % 2, [from_top, candidate])
        elif levels == 3:
            following = top
            theirs = after(theirs, top)
        else:
            theirs = after(theirs, following)
        passed, entered = climb(mine, theirs, factors)
        if level == levels - 1:
            near_upper_inv = swap(after(leaf_upper_inv, passed), "col", 1)
            near_upper_panels = swap(after(leaf_upper_panels, passed), "col", 1)
        held, following = hold(level, after(factors, passed), following, [*held, own, far] if level > 1 else [])
        mine, factors, own, far = passed, following, entered, swap(entered, "col", 2)
    theirs = swap(mine, "leaf", 2 ** (levels - 1))
    own_top = enter(mine, theirs)
    paths = descend(levels, own, far, own_top, swap(own_top, "col", 2), factors, *held)

    own_solution = jnp.zeros((size, cols), BF16)
    for level in range(levels):
        own_solution = jnp.where(owned[level], paths[level, :, :cols], own_solution)

    local = (ancestors, leaf_upper_inv, leaf_upper_panels)
    near = (near_ancestors, near_upper_inv, near_upper_panels)
    leaf_solution = solve_own(scalars, 0, *local, value_1, paths, rows)
    quarter = half // 2
    returning = [
        (3, 0, solve_far(*local, value_1, paths, 0, count - quarter)),
        (4, 0, solve_far(*near, value_2_far, paths, 0, half)),
        (4, half, solve_far(*near, value_2_far, paths, half, half)),
        (3, count - quarter, solve_far(*local, value_1, paths, count - quarter, quarter)),
    ]
    leaf_solution = solve_own(scalars, 1, *near, value_2_own, paths, rows, leaf_solution)
    for which, offset, part in returning:
        leaf_solution = place_rows(scalars, which, offset, swap(part, "col", 2), leaf_solution)
    return (leaf_solution, own_solution[None])


def solution(mesh):
    placed = (
        P("leaf", None, "col"),
        P(("leaf", "col"), None, None),
        P(("leaf", "col"), None, None, None),
        P(("leaf", "col"), None, None),
        P(("leaf", "col"), None, None, None),
        P(("leaf", "col"), None),
        P("leaf", None, "col"),
        P("leaf", None, None),
        P("leaf", None, None, None),
        P("leaf", None, None),
        P("leaf", None, None, None),
    )
    return jax.shard_map(
        on_device,
        mesh=mesh,
        in_specs=placed,
        out_specs=(P("leaf", None, "col"), P("leaf", None, "col")),
        check_vma=False,
    )
```

```python
import functools

import jax
import jax.numpy as jnp
from jax import lax
from jax.experimental import pallas as pl
from jax.experimental.pallas import tpu as pltpu
from jax.sharding import PartitionSpec as P

F32 = jnp.float32
BF16 = jnp.bfloat16
FORWARD_VMEM = 60 * 2**20
LEAF_VMEM = 10 * 2**20
TREE_VMEM = 6 * 2**20
BATCH = 4
SOLVE_BATCH = 6
PART = 3


def swap(value, axis, mask):
    pairs = [(source, source ^ mask) for source in range(lax.axis_size(axis))]
    return lax.ppermute(value, axis, pairs)


def dot(left, right):
    return jnp.dot(left, right, preferred_element_type=F32)


def cost(flops, moved):
    return pl.CostEstimate(flops=flops, bytes_accessed=moved, transcendentals=0)


def forward_kernel(own, far, first, scalars, ancestors, *refs):
    sides = own + far
    columns_in, (inv, panels, start) = refs[:sides], refs[sides : sides + 3]
    value, *totals = refs[sides + 3 : -3]
    solved, held, sems = refs[-3:]
    step, steps = pl.program_id(0), pl.num_programs(0)
    batch, slots = panels.shape[:2]
    levels = held.shape[0]
    cols = start.shape[2]

    def leaving(leaf):
        return pltpu.make_async_copy(solved.at[leaf], value.at[leaf], sems.at[leaf])

    @pl.when(step == 0)
    def _():
        if first:
            for level in range(levels):
                held[level] = start[0].astype(F32) * -(scalars[2] == level + 1).astype(F32)
        else:
            held[:, :, :cols] = start[...]
            if sides == 2:
                held[:, :, cols:] = jnp.zeros((levels, held.shape[1], cols), F32)

    values = []
    for leaf in range(batch):
        columns = [array[leaf] for array in columns_in]
        columns = jnp.concatenate(columns, axis=1) if sides == 2 else columns[0]
        values.append(dot(inv[leaf], columns).astype(BF16))
        solved[step * batch + leaf] = values[leaf]
        leaving(step * batch + leaf).start()
    sums = [None] * levels
    for leaf in range(batch):
        for slot in range(slots):
            product = dot(panels[leaf, slot], values[leaf])
            named = ancestors[step * batch + leaf, slot]
            for level in range(levels):
                term = product * (named == level + 1).astype(F32)
                sums[level] = term if sums[level] is None else sums[level] + term
    for level in range(levels):
        held[level] += sums[level]

    @pl.when(step == steps - 1)
    def _():
        for side, total in enumerate(totals):
            total[...] = held[:, :, side * cols : (side + 1) * cols].astype(total.dtype)
        for leaf in range(solved.shape[0]):
            leaving(leaf).wait()


def forward(levels, scalars, which, ancestors, inv, panels, rhs, far, start, first, types):
    count, size, _ = inv.shape
    cols = start.shape[2]
    slots = panels.shape[1]
    batch = min(BATCH, count)
    whole = lambda i, *_: (0, 0, 0)
    sides = [array for array in (rhs, far) if array is not None]
    specs = []
    if rhs is not None:
        specs.append(pl.BlockSpec((batch, size, cols), lambda i, scalars, _: (scalars[which] // batch + i, 0, 0)))
    if far is not None:
        specs.append(pl.BlockSpec((batch, size, cols), lambda i, *_: (i, 0, 0)))
    sums = [jax.ShapeDtypeStruct((levels, size, cols), kind) for kind in types]
    return pl.pallas_call(
        functools.partial(forward_kernel, rhs is not None, far is not None, first),
        grid_spec=pltpu.PrefetchScalarGridSpec(
            num_scalar_prefetch=2,
            grid=(count // batch,),
            in_specs=specs
            + [
                pl.BlockSpec((batch, size, size), lambda i, *_: (i, 0, 0)),
                pl.BlockSpec((batch, slots, size, size), lambda i, *_: (i, 0, 0, 0)),
                pl.BlockSpec(start.shape, whole),
            ],
            out_specs=[pl.BlockSpec(memory_space=pl.ANY)] + [pl.BlockSpec(part.shape, whole) for part in sums],
            scratch_shapes=[
                pltpu.VMEM((count, size, len(sides) * cols), BF16),
                pltpu.VMEM((levels, size, len(sides) * cols), F32),
                pltpu.SemaphoreType.DMA((count,)),
            ],
        ),
        out_shape=[jax.ShapeDtypeStruct((count, size, len(sides) * cols), BF16)] + sums,
        compiler_params=pltpu.CompilerParams(vmem_limit_bytes=FORWARD_VMEM),
        cost_estimate=cost(0, 0),
        name="leaf_forward",
    )(scalars, ancestors, *sides, inv, panels, start)


def solve_leaves(base, step, batch, ancestors, value, inv, panels, paths):
    leaves = [step * batch + index for index in range(batch)]
    rests = []
    for leaf in leaves:
        update = None
        for slot in range(panels.shape[1]):
            level = ancestors[base + leaf, slot]
            picked = paths[jnp.maximum(level - 1, 0)]
            picked = jnp.where(level > 0, picked, jnp.zeros_like(picked))
            term = dot(panels[leaf, slot], picked)
            update = term if update is None else update + term
        rests.append((value[leaf].astype(F32) - update).astype(BF16))
    return [dot(inv[leaf], rest).astype(BF16) for leaf, rest in zip(leaves, rests)]


def send_kernel(base, ancestors, value, inv, panels, paths, result):
    step = pl.program_id(0)
    batch = result.shape[0]
    solutions = solve_leaves(base + step * batch, 0, batch, ancestors, value, inv, panels, paths)
    for index, solution_block in enumerate(solutions):
        result[index] = solution_block


def solve_far(ancestors, inv, panels, value, paths, base, count):
    levels, size, cols = paths.shape[0], paths.shape[1], paths.shape[2] // 2
    batch = max(leaves for leaves in range(1, SOLVE_BATCH + 1) if count % leaves == 0 and base % leaves == 0)
    ahead = base // batch

    def part(array):
        block = (batch,) + array.shape[1:]
        return pl.BlockSpec(block, lambda i: (ahead + i,) + (0,) * (array.ndim - 1))

    return pl.pallas_call(
        functools.partial(send_kernel, base),
        grid=(count // batch,),
        in_specs=[
            pl.BlockSpec(memory_space=pltpu.SMEM),
            pl.BlockSpec((batch, size, cols), lambda i: (ahead + i, 0, value.shape[2] // cols - 1)),
            part(inv),
            part(panels),
            pl.BlockSpec((levels, size, cols), lambda i: (0, 0, 1)),
        ],
        out_specs=pl.BlockSpec((batch, size, cols), lambda i: (i, 0, 0)),
        out_shape=jax.ShapeDtypeStruct((count, size, cols), BF16),
        compiler_params=pltpu.CompilerParams(vmem_limit_bytes=LEAF_VMEM),
        cost_estimate=cost(0, 0),
        name="solve_far",
    )(ancestors, value, inv, panels, paths)


def keep_kernel(which, scalars, ancestors, value, inv, panels, paths, *refs):
    result, solved, sems = refs[-3:]
    step, steps = pl.program_id(0), pl.num_programs(0)
    batch = value.shape[0]

    def leaving(leaf):
        return pltpu.make_async_copy(solved.at[leaf], result.at[scalars[which] + leaf], sems.at[leaf])

    for index, solution_block in enumerate(solve_leaves(step * batch, 0, batch, ancestors, value, inv, panels, paths)):
        solved[step * batch + index] = solution_block
        leaving(step * batch + index).start()

    @pl.when(step == steps - 1)
    def _():
        for leaf in range(solved.shape[0]):
            leaving(leaf).wait()


def solve_own(scalars, which, ancestors, inv, panels, value, paths, rows, into=None):
    levels, size, cols = paths.shape[0], paths.shape[1], paths.shape[2] // 2
    count, slots = panels.shape[:2]
    batch = min(BATCH, count)
    extra = [] if into is None else [into]
    hbm, smem = pl.BlockSpec(memory_space=pl.ANY), pl.BlockSpec(memory_space=pltpu.SMEM)
    return pl.pallas_call(
        functools.partial(keep_kernel, which),
        grid=(count // batch,),
        in_specs=[
            smem,
            smem,
            pl.BlockSpec((batch, size, cols), lambda i: (i, 0, 0)),
            pl.BlockSpec((batch, size, size), lambda i: (i, 0, 0)),
            pl.BlockSpec((batch, slots, size, size), lambda i: (i, 0, 0, 0)),
            pl.BlockSpec((levels, size, cols), lambda i: (0, 0, 0)),
        ]
        + [hbm] * len(extra),
        out_specs=hbm,
        out_shape=jax.ShapeDtypeStruct((rows, size, cols), BF16),
        scratch_shapes=[pltpu.VMEM((count, size, cols), BF16), pltpu.SemaphoreType.DMA((count,))],
        input_output_aliases={} if into is None else {6: 0},
        compiler_params=pltpu.CompilerParams(vmem_limit_bytes=LEAF_VMEM),
        cost_estimate=cost(0, 0),
        name="solve_own",
    )(scalars, ancestors, value, inv, panels, paths, *extra)


def place_kernel(group, leaves, offset, part, whole, result, sem):
    place = lax.axis_index("col")
    row = (1 - place // 2) * 2 * leaves + (place + group) % 2 * leaves + offset
    copy = pltpu.make_async_copy(part, result.at[pl.ds(row, part.shape[0])], sem)
    copy.start()
    copy.wait()


def place_rows(group, leaves, offset, part, whole):
    hbm = pl.BlockSpec(memory_space=pl.ANY)
    return pl.pallas_call(
        functools.partial(place_kernel, group, leaves, offset),
        in_specs=[pl.BlockSpec(memory_space=pltpu.VMEM), hbm],
        out_specs=hbm,
        out_shape=jax.ShapeDtypeStruct(whole.shape, whole.dtype),
        scratch_shapes=[pltpu.SemaphoreType.DMA],
        input_output_aliases={1: 0},
        compiler_params=pltpu.CompilerParams(vmem_limit_bytes=LEAF_VMEM),
        cost_estimate=cost(0, 0),
        name="place_rows",
    )(part, whole)


def combine_kernel(lower_inv, lower_panels, upper_inv, upper_panels, blocks, *parts):
    made = [dot(upper_inv[0], lower_inv[0]).astype(BF16)]
    for slot in range(blocks.shape[0] // 2):
        made.append(dot(lower_panels[0, slot], lower_inv[0]).astype(BF16))
        made.append(dot(upper_inv[0], upper_panels[0, slot]).astype(BF16))
    for index, block in enumerate(made):
        blocks[index] = block
    for part in parts:
        for index in range(part.shape[0]):
            part[index] = made.pop(0)


def combine(lower_inv, lower_panels, upper_inv, upper_panels):
    size = lower_inv.shape[1]
    total = 1 + 2 * lower_panels.shape[1]
    counts = [total] + [min(PART, total - begin) for begin in range(0, total, PART)]
    blocks, *parts = pl.pallas_call(
        combine_kernel,
        out_shape=[jax.ShapeDtypeStruct((blocks, size, size), BF16) for blocks in counts],
        compiler_params=pltpu.CompilerParams(vmem_limit_bytes=TREE_VMEM),
        cost_estimate=cost(2**20, 2**20),
        name="combine",
    )(lower_inv, lower_panels, upper_inv, upper_panels)
    return blocks, parts


def sort_kernel(parts, wanted, flags, mine, *refs):
    theirs, chosen = refs[:parts], refs[parts:]

    @pl.when(flags[0] == wanted)
    def _():
        for out in chosen:
            out[...] = mine[: out.shape[0]]

    @pl.when(flags[0] != wanted)
    def _():
        for out in chosen:
            begin = 0
            for part in theirs:
                for index in range(min(part.shape[0], out.shape[0] - begin)):
                    out[begin + index] = part[index]
                begin += part.shape[0]


def sort(bit, wanted, mine, theirs, counts):
    memory = pl.BlockSpec(memory_space=pltpu.VMEM)
    return pl.pallas_call(
        functools.partial(sort_kernel, len(theirs), wanted),
        in_specs=[pl.BlockSpec(memory_space=pltpu.SMEM), memory] + [memory] * len(theirs),
        out_specs=[memory] * len(counts),
        out_shape=[jax.ShapeDtypeStruct((count,) + mine.shape[1:], BF16) for count in counts],
        compiler_params=pltpu.CompilerParams(vmem_limit_bytes=TREE_VMEM),
        cost_estimate=cost(2**20, 2**20),
        name="sort",
    )(jnp.reshape(bit, (1,)).astype(jnp.int32), mine, *theirs)


def pick_kernel(flags, *refs):
    sources, chosen, sem = refs[:-2], refs[-2], refs[-1]
    for index, source in enumerate(sources):

        @pl.when(flags[0] == index)
        def _(source=source):
            copy = pltpu.make_async_copy(source.at[:1], chosen, sem)
            copy.start()
            copy.wait()


def pick(index, sources):
    return pl.pallas_call(
        pick_kernel,
        in_specs=[pl.BlockSpec(memory_space=pltpu.SMEM)] + [pl.BlockSpec(memory_space=pl.ANY)] * len(sources),
        out_specs=pl.BlockSpec(memory_space=pltpu.VMEM),
        out_shape=jax.ShapeDtypeStruct((1,) + sources[0].shape[1:], BF16),
        scratch_shapes=[pltpu.SemaphoreType.DMA],
        compiler_params=pltpu.CompilerParams(vmem_limit_bytes=FORWARD_VMEM),
        cost_estimate=cost(2**20, 2**20),
        name="pick",
    )(jnp.reshape(index, (1,)).astype(jnp.int32), *sources)


def from_owners(value, level, hop):
    owner = 2 ** (level - 1)
    pairs = [
        (group + owner + index, group + (owner + index ^ hop))
        for group in range(0, lax.axis_size("leaf"), 2**level)
        for index in range(2)
    ]
    return lax.ppermute(value, "leaf", pairs)


def after(value, *earlier):
    return lax.optimization_barrier((value, *earlier))[0]


def climb_kernel(mine, theirs, factors, passed, entered):
    here = (-(mine[0].astype(F32) + theirs[0].astype(F32))).astype(BF16)
    for above in range(passed.shape[0]):
        carried = mine[above + 1].astype(F32) + theirs[above + 1].astype(F32)
        passed[above] = (carried + dot(factors[1 + 2 * above], here)).astype(BF16)
    entered[0] = here


def climb(mine, theirs, factors):
    levels, size, cols = mine.shape
    vmem = pl.BlockSpec(memory_space=pltpu.VMEM)
    return pl.pallas_call(
        climb_kernel,
        in_specs=[vmem] * 3,
        out_specs=[vmem] * 2,
        out_shape=[
            jax.ShapeDtypeStruct((levels - 1, size, cols), BF16),
            jax.ShapeDtypeStruct((1, size, cols), BF16),
        ],
        compiler_params=pltpu.CompilerParams(vmem_limit_bytes=TREE_VMEM),
        cost_estimate=cost(2**20, 2**20),
        name="climb",
    )(mine, theirs, factors)


def hold_kernel(below, factors, next_factors, *refs):
    refs, (kept, inputs, onward) = refs[:-3], refs[-3:]
    begin = 0
    if below == 1:
        begin = refs[0].shape[0]
        kept[:begin] = refs[0][...]
        cols = refs[2].shape[2]
        if inputs.shape[0] > 1:
            inputs[:-1] = refs[1][...]
        inputs[inputs.shape[0] - 1, :, :cols] = refs[2][0]
        inputs[inputs.shape[0] - 1, :, cols:] = refs[3][0]
    else:
        inputs[...] = jnp.zeros(inputs.shape, BF16)
    count = factors.shape[0] // 2
    for above in range(count):
        kept[begin + above] = factors[2 + 2 * above]
    kept[begin + count] = factors[0]
    onward[...] = next_factors[...]


def hold(level, factors, next_factors, before):
    size = factors.shape[1]
    vmem = pl.BlockSpec(memory_space=pltpu.VMEM)
    blocks = factors.shape[0] // 2 + 1 + (before[0].shape[0] if before else 0)
    cols = 2 * before[2].shape[2] if before else size
    *held, onward = pl.pallas_call(
        functools.partial(hold_kernel, len(before) // 4),
        in_specs=[vmem] * (2 + len(before)),
        out_specs=[vmem] * 3,
        out_shape=[
            jax.ShapeDtypeStruct((blocks, size, size), BF16),
            jax.ShapeDtypeStruct((max(level - 1, 1), size, cols), BF16),
            jax.ShapeDtypeStruct(next_factors.shape, BF16),
        ],
        compiler_params=pltpu.CompilerParams(vmem_limit_bytes=TREE_VMEM),
        cost_estimate=cost(2**20, 2**20),
        name="hold",
    )(factors, next_factors, *before)
    return held, onward


def enter_kernel(mine, theirs, entered):
    entered[0] = (-(mine[0].astype(F32) + theirs[0].astype(F32))).astype(BF16)


def enter(mine, theirs):
    vmem = pl.BlockSpec(memory_space=pltpu.VMEM)
    return pl.pallas_call(
        enter_kernel,
        in_specs=[vmem] * 2,
        out_specs=vmem,
        out_shape=jax.ShapeDtypeStruct(mine.shape, BF16),
        compiler_params=pltpu.CompilerParams(vmem_limit_bytes=TREE_VMEM),
        cost_estimate=cost(2**20, 2**20),
        name="enter",
    )(mine, theirs)


def descend_kernel(own, far, own_top, far_top, top, kept, inputs, paths):
    levels = paths.shape[0]
    paths[levels - 1] = dot(top[0], jnp.concatenate([own_top[0], far_top[0]], axis=1)).astype(BF16)
    end = kept.shape[0]
    for level in range(levels - 2, -1, -1):
        count = levels - 1 - level
        end -= count + 1
        if level == levels - 2:
            entered = jnp.concatenate([own[0], far[0]], axis=1)
        else:
            entered = inputs[level]
        rest = dot(kept[end + count], entered)
        for above in reversed(range(count)):
            rest = rest - dot(kept[end + above], paths[level + 1 + above])
        paths[level] = rest.astype(BF16)


def descend(levels, own, far, own_top, far_top, top, kept, inputs):
    _, size, cols = own.shape
    vmem = pl.BlockSpec(memory_space=pltpu.VMEM)
    return pl.pallas_call(
        descend_kernel,
        in_specs=[vmem] * 7,
        out_specs=vmem,
        out_shape=jax.ShapeDtypeStruct((levels, size, 2 * cols), BF16),
        compiler_params=pltpu.CompilerParams(vmem_limit_bytes=TREE_VMEM),
        cost_estimate=cost(2**20, 2**20),
        name="descend",
    )(own, far, own_top, far_top, top, kept, inputs)


def on_device(
    leaf_rhs,
    leaf_lower_inv,
    leaf_lower_panels,
    leaf_upper_inv,
    leaf_upper_panels,
    ancestors,
    sep_rhs,
    sep_lower_inv,
    sep_lower_panels,
    sep_upper_inv,
    sep_upper_panels,
):
    levels = lax.axis_size("leaf").bit_length() - 1
    device = lax.axis_index("leaf")
    place = lax.axis_index("col")
    low, high = place % 2, place // 2
    count = leaf_lower_inv.shape[0]
    rows, size, cols = leaf_rhs.shape

    first = high * 2 * count + low * count
    second = high * 2 * count + (1 - low) * count
    owned = [device % 2**level == 2 ** (level - 1) for level in range(1, levels + 1)]
    own_level = sum(jnp.where(is_owner, level, 0) for level, is_owner in enumerate(owned, 1))

    away = (1 - high) * 2 * count
    scalars = jnp.stack([first, second, own_level]).astype(jnp.int32)
    half = count // 2
    sent = [lax.dynamic_slice_in_dim(leaf_rhs, away + low * count, count, 0)]
    sent.append(lax.dynamic_slice_in_dim(after(leaf_rhs, sent[0]), away + (1 - low) * count, count, 0))
    far_rhs = [swap(part, "col", 2) for part in sent]

    near_ancestors = swap(ancestors, "col", 1)
    near_lower_inv = swap(after(leaf_lower_inv, sent[0]), "col", 1)
    near_lower_panels = swap(after(leaf_lower_panels, sent[0]), "col", 1)
    local = (ancestors, leaf_lower_inv, leaf_lower_panels)
    near = (near_ancestors, near_lower_inv, near_lower_panels)

    blocks, pieces = combine(after(sep_lower_inv, *sent), sep_lower_panels, sep_upper_inv, sep_upper_panels)

    start = after(sep_rhs, *near)
    value_2_own, total = forward(levels, scalars, 1, *near, leaf_rhs, None, start, True, [F32])
    value_1, own_total, total = forward(levels, scalars, 0, *local, leaf_rhs, far_rhs[0], total, False, [BF16, F32])
    arrived = [swap(piece, "leaf", 1) for piece in pieces]
    count_above = blocks.shape[0] - 2
    onward = sort(device % 2, 0, blocks, after(arrived, total), (count_above, 1)) if levels > 1 else []
    total = after(total, *onward)
    value_2_far, far_total = forward(levels, scalars, 1, *near, None, far_rhs[1], total, False, [BF16])

    if levels == 3:
        from_top = [from_owners(onward[1], levels, hop) for hop in (4, 6)]
        far_total = after(far_total, *from_top)
    mine = (own_total.astype(F32) + swap(far_total, "col", 2).astype(F32)).astype(BF16)
    if levels == 3:
        from_top = pick(device // 2 % 2, from_top)
        mine = after(mine, from_top)
    (factors,) = sort(device % 2, 1, blocks, after(arrived, mine), (blocks.shape[0],))
    held = []
    for level in range(1, levels):
        theirs = swap(mine, "leaf", 2 ** (level - 1))
        here = onward[0]
        if levels != 3 or level == 1:
            arrived = swap(here, "leaf", 2**level)
            (following,) = sort(device // 2**level % 2, 1, here, [arrived], (here.shape[0],))
        if level < levels - 1 and levels != 3:
            onward = sort(device // 2**level % 2, 0, here, [arrived], (here.shape[0] - 2, 1))
        if levels == 3 and level == 1:
            (candidate,) = sort(device // 2 % 2, 0, here, [arrived], (1,))
            theirs = after(theirs, following, candidate)
            top = pick(device // 4 % 2, [from_top, candidate])
        elif levels == 3:
            following = top
            theirs = after(theirs, top)
        else:
            theirs = after(theirs, following)
        passed, entered = climb(mine, theirs, factors)
        if level == levels - 1:
            near_upper_inv = swap(after(leaf_upper_inv, passed), "col", 1)
            near_upper_panels = swap(after(leaf_upper_panels, passed), "col", 1)
        held, following = hold(level, after(factors, passed), following, [*held, own, far] if level > 1 else [])
        mine, factors, own, far = passed, following, entered, swap(entered, "col", 2)
    theirs = swap(mine, "leaf", 2 ** (levels - 1))
    own_top = enter(mine, theirs)
    paths = descend(levels, own, far, own_top, swap(own_top, "col", 2), factors, *held)

    own_solution = jnp.zeros((size, cols), BF16)
    for level in range(levels):
        own_solution = jnp.where(owned[level], paths[level, :, :cols], own_solution)

    local = (ancestors, leaf_upper_inv, leaf_upper_panels)
    near = (near_ancestors, near_upper_inv, near_upper_panels)
    leaf_solution = solve_own(scalars, 0, *local, value_1, paths, rows)
    quarter = half // 2
    returning = [
        (0, 0, solve_far(*local, value_1, paths, 0, count - quarter)),
        (1, 0, solve_far(*near, value_2_far, paths, 0, half)),
        (1, half, solve_far(*near, value_2_far, paths, half, half)),
        (0, count - quarter, solve_far(*local, value_1, paths, count - quarter, quarter)),
    ]
    leaf_solution = solve_own(scalars, 1, *near, value_2_own, paths, rows, leaf_solution)
    for group, offset, part in returning:
        leaf_solution = place_rows(group, count, offset, swap(part, "col", 2), leaf_solution)
    return (leaf_solution, own_solution[None])


def solution(mesh):
    placed = (
        P("leaf", None, "col"),
        P(("leaf", "col"), None, None),
        P(("leaf", "col"), None, None, None),
        P(("leaf", "col"), None, None),
        P(("leaf", "col"), None, None, None),
        P(("leaf", "col"), None),
        P("leaf", None, "col"),
        P("leaf", None, None),
        P("leaf", None, None, None),
        P("leaf", None, None),
        P("leaf", None, None, None),
    )
    return jax.shard_map(
        on_device,
        mesh=mesh,
        in_specs=placed,
        out_specs=(P("leaf", None, "col"), P("leaf", None, "col")),
        check_vma=False,
    )
```

```python
import functools

import jax
import jax.numpy as jnp
from jax import lax
from jax.experimental import pallas as pl
from jax.experimental.pallas import tpu as pltpu
from jax.sharding import PartitionSpec as P

F32 = jnp.float32
BF16 = jnp.bfloat16
FORWARD_VMEM = 60 * 2**20
LEAF_VMEM = 10 * 2**20
TREE_VMEM = 6 * 2**20
BATCH = 4
SOLVE_BATCH = 6
PART = 3


def swap(value, axis, mask):
    pairs = [(source, source ^ mask) for source in range(lax.axis_size(axis))]
    return lax.ppermute(value, axis, pairs)


def dot(left, right):
    return jnp.dot(left, right, preferred_element_type=F32)


def cost(flops, moved):
    return pl.CostEstimate(flops=flops, bytes_accessed=moved, transcendentals=0)


def forward_kernel(own, far, first, scalars, ancestors, *refs):
    sides = own + far
    columns_in, (inv, panels, start) = refs[:sides], refs[sides : sides + 3]
    value, *totals = refs[sides + 3 : -3]
    solved, held, sems = refs[-3:]
    step, steps = pl.program_id(0), pl.num_programs(0)
    batch, slots = panels.shape[:2]
    levels = held.shape[0]
    cols = start.shape[2]

    def leaving(leaf):
        return pltpu.make_async_copy(solved.at[leaf], value.at[leaf], sems.at[leaf])

    @pl.when(step == 0)
    def _():
        if first:
            for level in range(levels):
                held[level] = start[0].astype(F32) * -(scalars[2] == level + 1).astype(F32)
        else:
            held[:, :, :cols] = start[...]
            if sides == 2:
                held[:, :, cols:] = jnp.zeros((levels, held.shape[1], cols), F32)

    values = []
    for leaf in range(batch):
        columns = [array[leaf] for array in columns_in]
        columns = jnp.concatenate(columns, axis=1) if sides == 2 else columns[0]
        values.append(dot(inv[leaf], columns).astype(BF16))
        solved[step * batch + leaf] = values[leaf]
        leaving(step * batch + leaf).start()
    sums = [None] * levels
    for leaf in range(batch):
        for slot in range(slots):
            product = dot(panels[leaf, slot], values[leaf])
            named = ancestors[step * batch + leaf, slot]
            for level in range(levels):
                term = product * (named == level + 1).astype(F32)
                sums[level] = term if sums[level] is None else sums[level] + term
    for level in range(levels):
        held[level] += sums[level]

    @pl.when(step == steps - 1)
    def _():
        for side, total in enumerate(totals):
            total[...] = held[:, :, side * cols : (side + 1) * cols].astype(total.dtype)
        for leaf in range(solved.shape[0]):
            leaving(leaf).wait()


def forward(levels, scalars, which, ancestors, inv, panels, rhs, far, start, first, types):
    count, size, _ = inv.shape
    cols = start.shape[2]
    slots = panels.shape[1]
    batch = min(BATCH, count)
    whole = lambda i, *_: (0, 0, 0)
    sides = [array for array in (rhs, far) if array is not None]
    specs = []
    if rhs is not None:
        specs.append(pl.BlockSpec((batch, size, cols), lambda i, scalars, _: (scalars[which] // batch + i, 0, 0)))
    if far is not None:
        specs.append(pl.BlockSpec((batch, size, cols), lambda i, *_: (i, 0, 0)))
    sums = [jax.ShapeDtypeStruct((levels, size, cols), kind) for kind in types]
    return pl.pallas_call(
        functools.partial(forward_kernel, rhs is not None, far is not None, first),
        grid_spec=pltpu.PrefetchScalarGridSpec(
            num_scalar_prefetch=2,
            grid=(count // batch,),
            in_specs=specs
            + [
                pl.BlockSpec((batch, size, size), lambda i, *_: (i, 0, 0)),
                pl.BlockSpec((batch, slots, size, size), lambda i, *_: (i, 0, 0, 0)),
                pl.BlockSpec(start.shape, whole),
            ],
            out_specs=[pl.BlockSpec(memory_space=pl.ANY)] + [pl.BlockSpec(part.shape, whole) for part in sums],
            scratch_shapes=[
                pltpu.VMEM((count, size, len(sides) * cols), BF16),
                pltpu.VMEM((levels, size, len(sides) * cols), F32),
                pltpu.SemaphoreType.DMA((count,)),
            ],
        ),
        out_shape=[jax.ShapeDtypeStruct((count, size, len(sides) * cols), BF16)] + sums,
        compiler_params=pltpu.CompilerParams(vmem_limit_bytes=FORWARD_VMEM),
        cost_estimate=cost(0, 0),
        name="leaf_forward",
    )(scalars, ancestors, *sides, inv, panels, start)


def solve_leaves(base, step, batch, ancestors, value, inv, panels, paths):
    leaves = [step * batch + index for index in range(batch)]
    rests = []
    for leaf in leaves:
        update = None
        for slot in range(panels.shape[1]):
            level = ancestors[base + leaf, slot]
            picked = paths[jnp.maximum(level - 1, 0)]
            picked = jnp.where(level > 0, picked, jnp.zeros_like(picked))
            term = dot(panels[leaf, slot], picked)
            update = term if update is None else update + term
        rests.append((value[leaf].astype(F32) - update).astype(BF16))
    return [dot(inv[leaf], rest).astype(BF16) for leaf, rest in zip(leaves, rests)]


def send_kernel(base, ancestors, value, inv, panels, paths, result):
    step = pl.program_id(0)
    batch = result.shape[0]
    solutions = solve_leaves(base + step * batch, 0, batch, ancestors, value, inv, panels, paths)
    for index, solution_block in enumerate(solutions):
        result[index] = solution_block


def solve_far(ancestors, inv, panels, value, paths, base, count):
    levels, size, cols = paths.shape[0], paths.shape[1], paths.shape[2] // 2
    batch = max(leaves for leaves in range(1, SOLVE_BATCH + 1) if count % leaves == 0 and base % leaves == 0)
    ahead = base // batch

    def part(array):
        block = (batch,) + array.shape[1:]
        return pl.BlockSpec(block, lambda i: (ahead + i,) + (0,) * (array.ndim - 1))

    return pl.pallas_call(
        functools.partial(send_kernel, base),
        grid=(count // batch,),
        in_specs=[
            pl.BlockSpec(memory_space=pltpu.SMEM),
            pl.BlockSpec((batch, size, cols), lambda i: (ahead + i, 0, value.shape[2] // cols - 1)),
            part(inv),
            part(panels),
            pl.BlockSpec((levels, size, cols), lambda i: (0, 0, 1)),
        ],
        out_specs=pl.BlockSpec((batch, size, cols), lambda i: (i, 0, 0)),
        out_shape=jax.ShapeDtypeStruct((count, size, cols), BF16),
        compiler_params=pltpu.CompilerParams(vmem_limit_bytes=LEAF_VMEM),
        cost_estimate=cost(0, 0),
        name="solve_far",
    )(ancestors, value, inv, panels, paths)


def keep_kernel(which, scalars, ancestors, value, inv, panels, paths, *refs):
    result, solved, sems = refs[-3:]
    step, steps = pl.program_id(0), pl.num_programs(0)
    batch = value.shape[0]

    def leaving(leaf):
        return pltpu.make_async_copy(solved.at[leaf], result.at[scalars[which] + leaf], sems.at[leaf])

    for index, solution_block in enumerate(solve_leaves(step * batch, 0, batch, ancestors, value, inv, panels, paths)):
        solved[step * batch + index] = solution_block
        leaving(step * batch + index).start()

    @pl.when(step == steps - 1)
    def _():
        for leaf in range(solved.shape[0]):
            leaving(leaf).wait()


def solve_own(scalars, which, ancestors, inv, panels, value, paths, rows, into=None):
    levels, size, cols = paths.shape[0], paths.shape[1], paths.shape[2] // 2
    count, slots = panels.shape[:2]
    batch = min(BATCH, count)
    extra = [] if into is None else [into]
    hbm, smem = pl.BlockSpec(memory_space=pl.ANY), pl.BlockSpec(memory_space=pltpu.SMEM)
    return pl.pallas_call(
        functools.partial(keep_kernel, which),
        grid=(count // batch,),
        in_specs=[
            smem,
            smem,
            pl.BlockSpec((batch, size, cols), lambda i: (i, 0, 0)),
            pl.BlockSpec((batch, size, size), lambda i: (i, 0, 0)),
            pl.BlockSpec((batch, slots, size, size), lambda i: (i, 0, 0, 0)),
            pl.BlockSpec((levels, size, cols), lambda i: (0, 0, 0)),
        ]
        + [hbm] * len(extra),
        out_specs=hbm,
        out_shape=jax.ShapeDtypeStruct((rows, size, cols), BF16),
        scratch_shapes=[pltpu.VMEM((count, size, cols), BF16), pltpu.SemaphoreType.DMA((count,))],
        input_output_aliases={} if into is None else {6: 0},
        compiler_params=pltpu.CompilerParams(vmem_limit_bytes=LEAF_VMEM),
        cost_estimate=cost(0, 0),
        name="solve_own",
    )(scalars, ancestors, value, inv, panels, paths, *extra)


def place_kernel(group, leaves, offset, part, whole, result, sem):
    place = lax.axis_index("col")
    row = (1 - place // 2) * 2 * leaves + (place + group) % 2 * leaves + offset
    copy = pltpu.make_async_copy(part, result.at[pl.ds(row, part.shape[0])], sem)
    copy.start()
    copy.wait()


def place_rows(group, leaves, offset, part, whole):
    hbm = pl.BlockSpec(memory_space=pl.ANY)
    return pl.pallas_call(
        functools.partial(place_kernel, group, leaves, offset),
        in_specs=[pl.BlockSpec(memory_space=pltpu.VMEM), hbm],
        out_specs=hbm,
        out_shape=jax.ShapeDtypeStruct(whole.shape, whole.dtype),
        scratch_shapes=[pltpu.SemaphoreType.DMA],
        input_output_aliases={1: 0},
        compiler_params=pltpu.CompilerParams(vmem_limit_bytes=LEAF_VMEM),
        cost_estimate=cost(0, 0),
        name="place_rows",
    )(part, whole)


def combine_kernel(lower_inv, lower_panels, upper_inv, upper_panels, blocks, *parts):
    made = [dot(upper_inv[0], lower_inv[0]).astype(BF16)]
    for slot in range(blocks.shape[0] // 2):
        made.append(dot(lower_panels[0, slot], lower_inv[0]).astype(BF16))
        made.append(dot(upper_inv[0], upper_panels[0, slot]).astype(BF16))
    for index, block in enumerate(made):
        blocks[index] = block
    for part in parts:
        for index in range(part.shape[0]):
            part[index] = made.pop(0)


def combine(lower_inv, lower_panels, upper_inv, upper_panels):
    size = lower_inv.shape[1]
    total = 1 + 2 * lower_panels.shape[1]
    counts = [total] + [min(PART, total - begin) for begin in range(0, total, PART)]
    blocks, *parts = pl.pallas_call(
        combine_kernel,
        out_shape=[jax.ShapeDtypeStruct((blocks, size, size), BF16) for blocks in counts],
        compiler_params=pltpu.CompilerParams(vmem_limit_bytes=TREE_VMEM),
        cost_estimate=cost(2**20, 2**20),
        name="combine",
    )(lower_inv, lower_panels, upper_inv, upper_panels)
    return blocks, parts


def sort_kernel(parts, wanted, flags, mine, *refs):
    theirs, chosen = refs[:parts], refs[parts:]

    @pl.when(flags[0] == wanted)
    def _():
        for out in chosen:
            out[...] = mine[: out.shape[0]]

    @pl.when(flags[0] != wanted)
    def _():
        for out in chosen:
            begin = 0
            for part in theirs:
                for index in range(min(part.shape[0], out.shape[0] - begin)):
                    out[begin + index] = part[index]
                begin += part.shape[0]


def sort(bit, wanted, mine, theirs, counts):
    memory = pl.BlockSpec(memory_space=pltpu.VMEM)
    return pl.pallas_call(
        functools.partial(sort_kernel, len(theirs), wanted),
        in_specs=[pl.BlockSpec(memory_space=pltpu.SMEM), memory] + [memory] * len(theirs),
        out_specs=[memory] * len(counts),
        out_shape=[jax.ShapeDtypeStruct((count,) + mine.shape[1:], BF16) for count in counts],
        compiler_params=pltpu.CompilerParams(vmem_limit_bytes=TREE_VMEM),
        cost_estimate=cost(2**20, 2**20),
        name="sort",
    )(jnp.reshape(bit, (1,)).astype(jnp.int32), mine, *theirs)


def pick_kernel(flags, *refs):
    sources, chosen, sem = refs[:-2], refs[-2], refs[-1]
    for index, source in enumerate(sources):

        @pl.when(flags[0] == index)
        def _(source=source):
            copy = pltpu.make_async_copy(source.at[:1], chosen, sem)
            copy.start()
            copy.wait()


def pick(index, sources):
    return pl.pallas_call(
        pick_kernel,
        in_specs=[pl.BlockSpec(memory_space=pltpu.SMEM)] + [pl.BlockSpec(memory_space=pl.ANY)] * len(sources),
        out_specs=pl.BlockSpec(memory_space=pltpu.VMEM),
        out_shape=jax.ShapeDtypeStruct((1,) + sources[0].shape[1:], BF16),
        scratch_shapes=[pltpu.SemaphoreType.DMA],
        compiler_params=pltpu.CompilerParams(vmem_limit_bytes=FORWARD_VMEM),
        cost_estimate=cost(2**20, 2**20),
        name="pick",
    )(jnp.reshape(index, (1,)).astype(jnp.int32), *sources)


def from_owners(value, level, hop):
    owner = 2 ** (level - 1)
    pairs = [
        (group + owner + index, group + (owner + index ^ hop))
        for group in range(0, lax.axis_size("leaf"), 2**level)
        for index in range(2)
    ]
    return lax.ppermute(value, "leaf", pairs)


def after(value, *earlier):
    return lax.optimization_barrier((value, *earlier))[0]


def climb_kernel(mine, theirs, factors, passed, entered):
    here = (-(mine[0].astype(F32) + theirs[0].astype(F32))).astype(BF16)
    for above in range(passed.shape[0]):
        carried = mine[above + 1].astype(F32) + theirs[above + 1].astype(F32)
        passed[above] = (carried + dot(factors[1 + 2 * above], here)).astype(BF16)
    entered[0] = here


def climb(mine, theirs, factors):
    levels, size, cols = mine.shape
    vmem = pl.BlockSpec(memory_space=pltpu.VMEM)
    return pl.pallas_call(
        climb_kernel,
        in_specs=[vmem] * 3,
        out_specs=[vmem] * 2,
        out_shape=[
            jax.ShapeDtypeStruct((levels - 1, size, cols), BF16),
            jax.ShapeDtypeStruct((1, size, cols), BF16),
        ],
        compiler_params=pltpu.CompilerParams(vmem_limit_bytes=TREE_VMEM),
        cost_estimate=cost(2**20, 2**20),
        name="climb",
    )(mine, theirs, factors)


def hold_kernel(below, factors, next_factors, *refs):
    refs, (kept, inputs, onward) = refs[:-3], refs[-3:]
    begin = 0
    if below == 1:
        begin = refs[0].shape[0]
        kept[:begin] = refs[0][...]
        cols = refs[2].shape[2]
        if inputs.shape[0] > 1:
            inputs[:-1] = refs[1][...]
        inputs[inputs.shape[0] - 1, :, :cols] = refs[2][0]
        inputs[inputs.shape[0] - 1, :, cols:] = refs[3][0]
    else:
        inputs[...] = jnp.zeros(inputs.shape, BF16)
    count = factors.shape[0] // 2
    for above in range(count):
        kept[begin + above] = factors[2 + 2 * above]
    kept[begin + count] = factors[0]
    onward[...] = next_factors[...]


def hold(level, factors, next_factors, before):
    size = factors.shape[1]
    vmem = pl.BlockSpec(memory_space=pltpu.VMEM)
    blocks = factors.shape[0] // 2 + 1 + (before[0].shape[0] if before else 0)
    cols = 2 * before[2].shape[2] if before else size
    *held, onward = pl.pallas_call(
        functools.partial(hold_kernel, len(before) // 4),
        in_specs=[vmem] * (2 + len(before)),
        out_specs=[vmem] * 3,
        out_shape=[
            jax.ShapeDtypeStruct((blocks, size, size), BF16),
            jax.ShapeDtypeStruct((max(level - 1, 1), size, cols), BF16),
            jax.ShapeDtypeStruct(next_factors.shape, BF16),
        ],
        compiler_params=pltpu.CompilerParams(vmem_limit_bytes=TREE_VMEM),
        cost_estimate=cost(2**20, 2**20),
        name="hold",
    )(factors, next_factors, *before)
    return held, onward


def enter_kernel(mine, theirs, entered):
    entered[0] = (-(mine[0].astype(F32) + theirs[0].astype(F32))).astype(BF16)


def enter(mine, theirs):
    vmem = pl.BlockSpec(memory_space=pltpu.VMEM)
    return pl.pallas_call(
        enter_kernel,
        in_specs=[vmem] * 2,
        out_specs=vmem,
        out_shape=jax.ShapeDtypeStruct(mine.shape, BF16),
        compiler_params=pltpu.CompilerParams(vmem_limit_bytes=TREE_VMEM),
        cost_estimate=cost(2**20, 2**20),
        name="enter",
    )(mine, theirs)


def descend_kernel(own, far, own_top, far_top, top, kept, inputs, paths):
    levels = paths.shape[0]
    paths[levels - 1] = dot(top[0], jnp.concatenate([own_top[0], far_top[0]], axis=1)).astype(BF16)
    end = kept.shape[0]
    for level in range(levels - 2, -1, -1):
        count = levels - 1 - level
        end -= count + 1
        if level == levels - 2:
            entered = jnp.concatenate([own[0], far[0]], axis=1)
        else:
            entered = inputs[level]
        rest = dot(kept[end + count], entered)
        for above in reversed(range(count)):
            rest = rest - dot(kept[end + above], paths[level + 1 + above])
        paths[level] = rest.astype(BF16)


def descend(levels, own, far, own_top, far_top, top, kept, inputs):
    _, size, cols = own.shape
    vmem = pl.BlockSpec(memory_space=pltpu.VMEM)
    return pl.pallas_call(
        descend_kernel,
        in_specs=[vmem] * 7,
        out_specs=vmem,
        out_shape=jax.ShapeDtypeStruct((levels, size, 2 * cols), BF16),
        compiler_params=pltpu.CompilerParams(vmem_limit_bytes=TREE_VMEM),
        cost_estimate=cost(2**20, 2**20),
        name="descend",
    )(own, far, own_top, far_top, top, kept, inputs)


def on_device(
    leaf_rhs,
    leaf_lower_inv,
    leaf_lower_panels,
    leaf_upper_inv,
    leaf_upper_panels,
    ancestors,
    sep_rhs,
    sep_lower_inv,
    sep_lower_panels,
    sep_upper_inv,
    sep_upper_panels,
):
    levels = lax.axis_size("leaf").bit_length() - 1
    device = lax.axis_index("leaf")
    place = lax.axis_index("col")
    low, high = place % 2, place // 2
    count = leaf_lower_inv.shape[0]
    rows, size, cols = leaf_rhs.shape

    first = high * 2 * count + low * count
    second = high * 2 * count + (1 - low) * count
    owned = [device % 2**level == 2 ** (level - 1) for level in range(1, levels + 1)]
    own_level = sum(jnp.where(is_owner, level, 0) for level, is_owner in enumerate(owned, 1))

    away = (1 - high) * 2 * count
    scalars = jnp.stack([first, second, own_level]).astype(jnp.int32)
    half = count // 2
    sent = [lax.dynamic_slice_in_dim(leaf_rhs, away + low * count, count, 0)]
    sent.append(lax.dynamic_slice_in_dim(after(leaf_rhs, sent[0]), away + (1 - low) * count, count, 0))
    far_rhs = [swap(part, "col", 2) for part in sent]

    near_ancestors = swap(ancestors, "col", 1)
    near_lower_inv = swap(after(leaf_lower_inv, sent[0]), "col", 1)
    near_lower_panels = swap(after(leaf_lower_panels, sent[0]), "col", 1)
    local = (ancestors, leaf_lower_inv, leaf_lower_panels)
    near = (near_ancestors, near_lower_inv, near_lower_panels)

    blocks, pieces = combine(after(sep_lower_inv, *sent), sep_lower_panels, sep_upper_inv, sep_upper_panels)

    start = after(sep_rhs, *near)
    value_2_own, total = forward(levels, scalars, 1, *near, leaf_rhs, None, start, True, [F32])
    value_1, own_total, total = forward(levels, scalars, 0, *local, leaf_rhs, far_rhs[0], total, False, [BF16, F32])
    arrived = [swap(piece, "leaf", 1) for piece in pieces]
    count_above = blocks.shape[0] - 2
    onward = sort(device % 2, 0, blocks, after(arrived, total), (count_above, 1)) if levels > 1 else []
    total = after(total, *onward)
    value_2_far, far_total = forward(levels, scalars, 1, *near, None, far_rhs[1], total, False, [BF16])

    if levels == 3:
        from_top = [from_owners(onward[1], levels, hop) for hop in (4, 6)]
        far_total = after(far_total, *from_top)
    mine = (own_total.astype(F32) + swap(far_total, "col", 2).astype(F32)).astype(BF16)
    if levels == 3:
        from_top = pick(device // 2 % 2, from_top)
        mine = after(mine, from_top)
    (factors,) = sort(device % 2, 1, blocks, after(arrived, mine), (blocks.shape[0],))
    held = []
    for level in range(1, levels):
        theirs = swap(mine, "leaf", 2 ** (level - 1))
        here = onward[0]
        if levels != 3 or level == 1:
            arrived = swap(here, "leaf", 2**level)
            (following,) = sort(device // 2**level % 2, 1, here, [arrived], (here.shape[0],))
        if level < levels - 1 and levels != 3:
            onward = sort(device // 2**level % 2, 0, here, [arrived], (here.shape[0] - 2, 1))
        if levels == 3 and level == 1:
            (candidate,) = sort(device // 2 % 2, 0, here, [arrived], (1,))
            theirs = after(theirs, following, candidate)
            top = pick(device // 4 % 2, [from_top, candidate])
        elif levels == 3:
            following = top
            theirs = after(theirs, top)
        else:
            theirs = after(theirs, following)
        passed, entered = climb(mine, theirs, factors)
        if level == levels - 1:
            near_upper_inv = swap(after(leaf_upper_inv, passed), "col", 1)
            near_upper_panels = swap(after(leaf_upper_panels, passed), "col", 1)
        held, following = hold(level, after(factors, passed), following, [*held, own, far] if level > 1 else [])
        mine, factors, own, far = passed, following, entered, swap(entered, "col", 2)
    theirs = swap(mine, "leaf", 2 ** (levels - 1))
    own_top = enter(mine, theirs)
    paths = descend(levels, own, far, own_top, swap(own_top, "col", 2), factors, *held)

    own_solution = jnp.zeros((size, cols), BF16)
    for level in range(levels):
        own_solution = jnp.where(owned[level], paths[level, :, :cols], own_solution)

    local = (ancestors, leaf_upper_inv, leaf_upper_panels)
    near = (near_ancestors, near_upper_inv, near_upper_panels)
    leaf_solution = solve_own(scalars, 0, *local, value_1, paths, rows)
    rest = half - 1
    returning = [
        (0, 0, solve_far(*local, value_1, paths, 0, count - rest)),
        (1, 0, solve_far(*near, value_2_far, paths, 0, half)),
        (1, half, solve_far(*near, value_2_far, paths, half, half)),
        (0, count - rest, solve_far(*local, value_1, paths, count - rest, rest)),
    ]
    leaf_solution = solve_own(scalars, 1, *near, value_2_own, paths, rows, leaf_solution)
    for group, offset, part in returning:
        leaf_solution = place_rows(group, count, offset, swap(part, "col", 2), leaf_solution)
    return (leaf_solution, own_solution[None])


def solution(mesh):
    placed = (
        P("leaf", None, "col"),
        P(("leaf", "col"), None, None),
        P(("leaf", "col"), None, None, None),
        P(("leaf", "col"), None, None),
        P(("leaf", "col"), None, None, None),
        P(("leaf", "col"), None),
        P("leaf", None, "col"),
        P("leaf", None, None),
        P("leaf", None, None, None),
        P("leaf", None, None),
        P("leaf", None, None, None),
    )
    return jax.shard_map(
        on_device,
        mesh=mesh,
        in_specs=placed,
        out_specs=(P("leaf", None, "col"), P("leaf", None, "col")),
        check_vma=False,
    )
```
